32 devices in a mesh: batch: 8 (over z, y), rows: 4 (over x, core).
Axes of the slice: x: 2, y: 2, z: 4, core: 2. Of those that a mesh axis runs over, the one named last changes fastest.
Arguments:
- frames: bfloat16 [8, 4, 16, 64, 128], P('batch', None, None, 'rows'), may hold values from -6 to 6
- crop_sizes: int32 [8, 2], P('batch'), may hold values from 8 to 128, as said below
- kernel: float32 [1296, 512], P(None, ('batch', 'rows')), may hold values from -0.5 to 0.5
- gate_bias: float32 [512], P(('batch', 'rows')), may hold values from -0.3 to 0.3
- peepholes: float32 [3, 128], P(None, 'batch'), may hold values from -0.6 to 0.6
- cotangent: bfloat16 [8, 4, 64, 128, 128], P('batch', None, 'rows'), may hold values from -6 to 6
- kernel_first: float32 [1296, 512], P(None, ('batch', 'rows')), as said below
- kernel_second: float32 [1296, 512], P(None, ('batch', 'rows')), as said below
- bias_first: float32 [512], P(('batch', 'rows')), as said below
- bias_second: float32 [512], P(('batch', 'rows')), as said below
- peep_first: float32 [3, 128], P(None, 'batch'), as said below
- peep_second: float32 [3, 128], P(None, 'batch'), as said below
Outputs:
- hidden_seq: bfloat16 [8, 4, 64, 128, 128], P('batch', None, 'rows')
- frames_grad: float32 [8, 4, 16, 64, 128], P('batch', None, None, 'rows')
- grad_norm: float32 [], replicated
- kernel_new: float32 [1296, 512], P(None, ('batch', 'rows'))
- kernel_first_new: float32 [1296, 512], P(None, ('batch', 'rows'))
- kernel_second_new: float32 [1296, 512], P(None, ('batch', 'rows'))
- bias_new: float32 [512], P(('batch', 'rows'))
- bias_first_new: float32 [512], P(('batch', 'rows'))
- bias_second_new: float32 [512], P(('batch', 'rows'))
- peep_new: float32 [3, 128], P(None, 'batch')
- peep_first_new: float32 [3, 128], P(None, 'batch')
- peep_second_new: float32 [3, 128], P(None, 'batch')
The draws below stay inside these ranges and needn't reach their ends.
Inputs may be any that keep to these rules, and one draw needn't show every extreme that they name: `crop_sizes`: column 0 is a crop's height, column 1 its width; in every draw some crop has height 64 and some crop width 128. `kernel_first`: both signs. `kernel_second`: positive. `bias_first`: both signs. `bias_second`: positive. `peep_first`: both signs. `peep_second`: positive.
All inputs are finite; a program needn't handle non-finite values.
Results may differ from the reference program's by a relative error of at most 0.0078.
The reference program's roundings to bfloat16 on the way count: a program that leaves them out, or rounds other values in their place, can miss the bound.
Values may be sent and summed in bfloat16 or wider, within the bound.
A program may use at most 192 MiB of HBM per device.

```python
import math
import jax
import jax.numpy as jnp
from jax import lax

CIN = 16
HID = 128
GATES = 512
KROWS = 1296
WID = 128
FRAMES = 4
STEP = 5
HGT = 64
ITEMS = 8


GRAD_CLIP = 0.02


def entry_scale(factor):
    param_count = KROWS * GATES + GATES + 3 * HID
    return factor * GRAD_CLIP / math.sqrt(param_count)


def first_draw(subkey, array_shape, factor):
    return 0.111 * entry_scale(factor) * jax.random.normal(subkey, array_shape, jnp.float32)


def second_draw(subkey, array_shape, factor):
    spread = jnp.exp(jax.random.uniform(subkey, array_shape, jnp.float32, math.log(0.5), math.log(8.0)))
    magnitude = entry_scale(factor)
    return 0.001 * magnitude * magnitude * spread


def draw_crop_sizes(key, part):
    key = jax.random.fold_in(key, 3)
    key_height, key_width, key_tall, key_broad = jax.random.split(key, 4)
    heights = jax.random.randint(key_height, (ITEMS,), max(1, HGT // 8), HGT + 1)
    widths = jax.random.randint(key_width, (ITEMS,), max(1, WID // 8), WID + 1)
    tallest = jax.random.randint(key_tall, (), 0, ITEMS)
    broadest = jax.random.randint(key_broad, (), 0, ITEMS)
    positions = jnp.arange(ITEMS)
    heights = jnp.where(positions == tallest, HGT, heights)
    widths = jnp.where(positions == broadest, WID, widths)
    return jnp.stack([heights, widths], axis=1).astype(jnp.int32)


def draw_kernel_first(key, part):
    key = jax.random.fold_in(key, 11)
    return first_draw(key, (KROWS, GATES), 1.0)


def draw_kernel_second(key, part):
    key = jax.random.fold_in(key, 12)
    return second_draw(key, (KROWS, GATES), 1.0)


def draw_bias_first(key, part):
    key = jax.random.fold_in(key, 13)
    return first_draw(key, (GATES,), 3.0)


def draw_bias_second(key, part):
    key = jax.random.fold_in(key, 14)
    return second_draw(key, (GATES,), 3.0)


def draw_peep_first(key, part):
    key = jax.random.fold_in(key, 15)
    return first_draw(key, (3, HID), 1.0)


def draw_peep_second(key, part):
    key = jax.random.fold_in(key, 16)
    return second_draw(key, (3, HID), 1.0)


def levels(key, shape, cuts, low, top_value):
    loudness, own = 1.0, jax.random.fold_in(key, 6)
    for position, blocks in cuts:
        draws = jnp.exp(jax.random.uniform(jax.random.fold_in(own, position), (blocks,), jnp.float32, low / len(cuts), top_value / len(cuts)))
        loudness = loudness * jnp.repeat(draws, shape[position] // blocks).reshape([-1 if axis == position else 1 for axis in range(len(shape))])
    return loudness


def centred(stream_key, shape, deviation, limit, pieces=(), held_as=jnp.bfloat16):
    gain = levels(stream_key, shape, pieces, -0.22, 0.18) if pieces else 1.0
    array = jax.random.normal(stream_key, shape, jnp.float32) * deviation * gain
    return jnp.minimum(jnp.maximum(array, -limit), limit).astype(held_as)


def setup_inputs(seed: int = 0) -> dict:
    key_of = jax.random.split(jax.random.key(seed), 13)
    frames = centred(key_of[0], (ITEMS, FRAMES, CIN, HGT, WID), 1.0, 6.0, ((0, 8), (3, 4)))
    crop_sizes = draw_crop_sizes(jax.random.fold_in(key_of[12], 71), 0)
    kernel = centred(key_of[2], (KROWS, GATES), (9 * CIN) ** -0.5, 0.5, ((1, 32),), jnp.float32)
    gate_bias = centred(key_of[3], (GATES,), 0.05, 0.3, ((0, 32),), jnp.float32)
    peepholes = centred(key_of[4], (3, HID), 0.1, 0.6, ((1, 8),), jnp.float32)
    cotangent = centred(key_of[5], (ITEMS, FRAMES, HGT, WID, HID), 1.0, 6.0, ((0, 8), (2, 4)))
    kernel_first = draw_kernel_first(jax.random.fold_in(key_of[12], 71), 0)
    kernel_second = draw_kernel_second(jax.random.fold_in(key_of[12], 71), 0)
    bias_first = draw_bias_first(jax.random.fold_in(key_of[12], 71), 0)
    bias_second = draw_bias_second(jax.random.fold_in(key_of[12], 71), 0)
    peep_first = draw_peep_first(jax.random.fold_in(key_of[12], 71), 0)
    peep_second = draw_peep_second(jax.random.fold_in(key_of[12], 71), 0)
    return dict(frames=frames, crop_sizes=crop_sizes, kernel=kernel, gate_bias=gate_bias, peepholes=peepholes, cotangent=cotangent, kernel_first=kernel_first, kernel_second=kernel_second, bias_first=bias_first, bias_second=bias_second, peep_first=peep_first, peep_second=peep_second)


@jax.custom_vjp
def low(v):
    return lax.optimization_barrier(v.astype(jnp.bfloat16)).astype(jnp.float32)

@jax.custom_vjp
def low_back(v):
    return v

def low_keep(v):
    return (low(v), None)

def low_pass(kept, grad):
    return (grad,)

def back_keep(v):
    return (v, None)

def back_low(kept, grad):
    return (low(grad),)
low.defvjp(low_keep, low_pass)
low_back.defvjp(back_keep, back_low)
HIGHEST = lax.Precision.HIGHEST
CLIP_AT = 0.02
LEARN_RATE = 0.02
BETA_ONE = 0.9
BETA_TWO = 0.999
WEIGHT_DECAY = 0.01
ADAM_EPS = 1e-08

def crop_inside(sizes_item):
    rows_at = lax.broadcasted_iota(jnp.int32, (HGT, WID), 0)
    cols_at = lax.broadcasted_iota(jnp.int32, (HGT, WID), 1)
    return ((rows_at < sizes_item[0]) & (cols_at < sizes_item[1])).astype(jnp.float32)

def item_forward(frames_item, sizes_item, kernel_in, bias_in, peep_in):
    inside = crop_inside(sizes_item)
    weights = low(kernel_in).reshape(9, CIN + HID, GATES)

    def advance(carried, picture):
        hidden_state, cell_state = carried
        masked = jnp.transpose(picture * inside, (1, 2, 0))
        joined = jnp.concatenate([masked, hidden_state], axis=-1)
        padded = jnp.pad(joined, ((1, 1), (1, 1), (0, 0)))
        summed = jnp.zeros((HGT, WID, GATES), jnp.float32)
        for tap_index in range(9):
            row_shift = tap_index // 3
            col_shift = tap_index % 3
            window = padded[row_shift:row_shift + HGT, col_shift:col_shift + WID]
            summed = summed + jnp.einsum('hwc,cg->hwg', window, weights[tap_index], precision=HIGHEST)
        preact = low_back(summed) + bias_in
        in_gate = jax.nn.sigmoid(preact[..., :HID] + peep_in[0] * cell_state)
        forget = jax.nn.sigmoid(preact[..., HID:2 * HID] + peep_in[1] * cell_state)
        candidate = jnp.tanh(preact[..., 2 * HID:3 * HID])
        cell_next = inside[..., None] * (forget * cell_state + in_gate * candidate)
        out_gate = jax.nn.sigmoid(preact[..., 3 * HID:] + peep_in[2] * cell_next)
        state_next = low(inside[..., None] * out_gate * jnp.tanh(cell_next))
        return ((state_next, cell_next), state_next)
    zeros_state = jnp.zeros((HGT, WID, HID), jnp.float32)
    finished, states = lax.scan(jax.checkpoint(advance), (zeros_state, zeros_state), frames_item)
    return states

def adamw_update(weight, gradient, first, second, scale):
    clipped = gradient * scale
    first_new = BETA_ONE * first + (1.0 - BETA_ONE) * clipped
    second_new = BETA_TWO * second + (1.0 - BETA_TWO) * clipped * clipped
    first_hat = first_new / (1.0 - BETA_ONE ** STEP)
    second_hat = second_new / (1.0 - BETA_TWO ** STEP)
    weight_new = weight - LEARN_RATE * (first_hat / (jnp.sqrt(second_hat) + ADAM_EPS) + WEIGHT_DECAY * weight)
    return (weight_new, first_new, second_new)

def reference(frames, crop_sizes, kernel, gate_bias, peepholes, cotangent, kernel_first, kernel_second, bias_first, bias_second, peep_first, peep_second):
    frames_wide = frames.astype(jnp.float32)

    def forward(frames_in, kernel_in, bias_in, peep_in):

        def one_item(couple):
            return item_forward(couple[0], couple[1], kernel_in, bias_in, peep_in)
        return lax.map(jax.checkpoint(one_item), (frames_in, crop_sizes))
    hidden_seq, pullback = jax.vjp(forward, frames_wide, kernel, gate_bias, peepholes)
    frames_grad, kernel_grad, bias_grad, peep_grad = pullback(cotangent.astype(jnp.float32))
    squares = jnp.sum(kernel_grad * kernel_grad) + jnp.sum(bias_grad * bias_grad) + jnp.sum(peep_grad * peep_grad)
    grad_norm = jnp.sqrt(squares)
    scale = jnp.minimum(1.0, CLIP_AT / (grad_norm + 1e-06))
    kernel_new, kernel_first_new, kernel_second_new = adamw_update(kernel, kernel_grad, kernel_first, kernel_second, scale)
    bias_new, bias_first_new, bias_second_new = adamw_update(gate_bias, bias_grad, bias_first, bias_second, scale)
    peep_new, peep_first_new, peep_second_new = adamw_update(peepholes, peep_grad, peep_first, peep_second, scale)
    return (hidden_seq.astype(jnp.bfloat16), frames_grad, grad_norm, kernel_new, kernel_first_new, kernel_second_new, bias_new, bias_first_new, bias_second_new, peep_new, peep_first_new, peep_second_new)
```

```python
import functools
import math

import jax
import jax.numpy as jnp
from jax import lax
from jax.experimental import pallas as pl
from jax.experimental.pallas import tpu as pltpu
from jax.sharding import PartitionSpec as P

CIN = 16
HID = 128
GATES = 512
KROWS = 1296
WID = 128
STEP = 5
CLIP_AT = 0.02
LEARN_RATE = 0.02
BETA_ONE = 0.9
BETA_TWO = 0.999
WEIGHT_DECAY = 0.01
ADAM_EPS = 1e-08

F32 = jnp.float32
BF16 = jnp.bfloat16
MESH = pl.DeviceIdType.MESH
NT = (((1,), (1,)), ((), ()))
NN = (((1,), (0,)), ((), ()))

WIDE = 3 * HID
HALL = 3 * WIDE
FEAT = 3 * CIN
FPAD = 256
KALL = HALL + FPAD
SUB = 32
UNIT = 16


def sigmoid(v):
    return 0.5 * jnp.tanh(0.5 * v) + 0.5


def mm(a, b, dims):
    return lax.dot_general(a, b, dims, preferred_element_type=F32)


def layer_kernel(
    dims,
    crop_ref,
    frames_ref,
    kt_ref,
    small_ref,
    cot_hbm,
    hid_hbm,
    fg_ref,
    grad_ref,
    small_out,
    norm_out,
    wt,
    wft,
    fr,
    xt,
    sc,
    gates,
    cells,
    gpre,
    gcell,
    gs,
    ybuf,
    fgb,
    cot,
    hlast,
    srow,
    consts,
    sums,
    acc,
    facc,
    fhalo_s,
    fhalo_r,
    shalo_r,
    ghalo_s,
    ghalo_r,
    bhalo_s,
    bhalo_r,
    nat,
    sm1,
    sm2,
    *rest,
):
    nbat, nrow, frames_n, rows_n, hi_bits, lo_bits = dims
    pix = rows_n * WID
    rest = list(rest)
    stage_send = [rest.pop(0) for _ in range(4 * hi_bits)]
    stage_recv = [rest.pop(0) for _ in range(4 * hi_bits)]
    last_send = [rest.pop(0) for _ in range(4)]
    last_recv = [rest.pop(0) for _ in range(4)]
    lo_send = [rest.pop(0) for _ in range(lo_bits)]
    lo_recv = [rest.pop(0) for _ in range(2 * lo_bits)]
    sems = rest.pop(0)
    rsems = rest.pop(0)
    lsems = rest.pop(0)

    at_b = lax.axis_index("batch")
    at_r = lax.axis_index("rows")
    counter = [0]
    pending = []

    def remote(src, dst, bat, row):
        i = counter[0]
        counter[0] += 1
        c = pltpu.make_async_remote_copy(
            src_ref=src, dst_ref=dst, send_sem=sems.at[i], recv_sem=rsems.at[i],
            device_id=(bat, row), device_id_type=MESH,
        )
        c.start()
        pending.append(c)
        return c

    def bit_of(s):
        return (at_r // (1 << s)) % 2

    def partner(s):
        return at_r + (1 - 2 * bit_of(s)) * (1 << s)

    barrier = pltpu.get_barrier_semaphore()
    for k in range(1, nrow):
        pl.semaphore_signal(barrier, inc=1, device_id=(at_b, lax.rem(at_r + k, nrow)), device_id_type=MESH)
    for k in range(1, nbat):
        pl.semaphore_signal(barrier, inc=1, device_id=(lax.rem(at_b + k, nbat), at_r), device_id_type=MESH)

    cot_copy = pltpu.make_async_copy(cot_hbm.at[0], cot, lsems.at[0])
    cot_copy.start()

    ktv = kt_ref[...]
    own = []
    for tap in range(9):
        own.append(ktv[:, tap * (CIN + HID) + CIN : (tap + 1) * (CIN + HID)])
    for tap in range(9):
        own.append(ktv[:, tap * (CIN + HID) : tap * (CIN + HID) + CIN])
    own.append(jnp.zeros((UNIT, FPAD - 9 * CIN), F32))
    own = jnp.concatenate(own, axis=1).astype(BF16)

    hi = [bit_of(lo_bits + hi_bits - 1 - s) for s in range(hi_bits)]
    wt[(at_b, *hi)] = own
    sm1[0, at_r] = small_ref[...]
    pl.semaphore_wait(barrier, nrow - 1 + nbat - 1)

    def small_rows(i):
        return [
            remote(sm1.at[i, at_r], sm1.at[i, at_r], at_b, lax.rem(at_r + k, nrow)) for k in range(1, nrow)
        ]

    def small_batch(i, first):
        for c in first:
            c.wait_recv()
        total = sm1[i, 0]
        for k in range(1, nrow):
            total = total + sm1[i, k]
        sm2[i, at_b] = total
        return [
            remote(sm2.at[i, at_b], sm2.at[i, at_b], lax.rem(at_b + k, nbat), at_r) for k in range(1, nbat)
        ]

    def small_done(i, second):
        for c in second:
            c.wait_recv()
        total = sm2[i, 0]
        for k in range(1, nbat):
            total = total + sm2[i, k]
        return total

    lanes = [(HALL, KALL), (0, HALL)]

    def gather_low():
        for s in range(lo_bits):
            dst = lo_recv[lo_bits + s]
            src = lo_send[s]
            src[...] = wt[(at_b, *hi)].astype(BF16)
            c = remote(src, dst, at_b, partner(s))
            c.wait_recv()
            wt[(at_b, *hi)] = wt[(at_b, *hi)] + dst[...]

    def gather_batch(part):
        lo, up = lanes[part]
        ref = wt.at[(at_b, *hi, slice(None), pl.ds(lo, up - lo))]
        return [remote(ref, ref, lax.rem(at_b + k, nbat), at_r) for k in range(1, nbat)]

    def gather_rows(part, s):
        lo, up = lanes[part]
        n_own = hi_bits - s
        idx = (slice(None),) + (slice(None),) * s + tuple(hi[s:]) + (slice(None), pl.ds(lo, up - lo))
        ref = wt.at[idx]
        del n_own
        return remote(ref, ref, at_b, partner(lo_bits + hi_bits - 1 - s))

    gather_low()
    first = small_rows(0)
    g_batch = [gather_batch(p) for p in range(2)]

    crop_h = crop_ref[0, 0]
    crop_w = crop_ref[0, 1]
    row0 = at_r * rows_n
    has_up = (at_r > 0).astype(F32)
    has_down = (at_r < nrow - 1).astype(F32)
    up_r = lax.rem(at_r + nrow - 1, nrow)
    down_r = lax.rem(at_r + 1, nrow)

    rr3 = lax.broadcasted_iota(jnp.int32, (CIN, rows_n, WID), 1) + row0
    cc3 = lax.broadcasted_iota(jnp.int32, (CIN, rows_n, WID), 2)
    live3 = (rr3 < crop_h) & (cc3 < crop_w)
    for t in range(frames_n):
        masked = jnp.where(live3, frames_ref[0, t].astype(F32), 0.0)
        fr[t, 1 : rows_n + 1] = jnp.swapaxes(masked, 0, 1)
        fhalo_s[0, t] = fr[t, 1].astype(BF16)
        fhalo_s[1, t] = fr[t, rows_n].astype(BF16)
    f_up = remote(fhalo_s.at[0], fhalo_r.at[1], at_b, up_r)
    f_down = remote(fhalo_s.at[1], fhalo_r.at[0], at_b, down_r)

    lane = lax.broadcasted_iota(jnp.int32, (CIN, WID), 1)

    def lane_shift(v, by):
        at = lax.broadcasted_iota(jnp.int32, v.shape, 1)
        if by > 0:
            return jnp.where(at == WID - 1, 0.0, pltpu.roll(v, WID - 1, 1))
        return jnp.where(at == 0, 0.0, pltpu.roll(v, 1, 1))

    def row_shift(v, by):
        at = lax.broadcasted_iota(jnp.int32, v.shape, 0)
        if by > 0:
            return jnp.where(at == WID - 1, 0.0, pltpu.roll(v, WID - 1, 0))
        return jnp.where(at == 0, 0.0, pltpu.roll(v, 1, 0))

    def frame_cols(t, rr):
        v = fr[t, rr]
        three = jnp.concatenate([lane_shift(v, -1), v, lane_shift(v, 1)], axis=0)
        xt[t, WIDE : WIDE + FEAT, pl.ds(pl.multiple_of(rr * WID, WID), WID)] = three.astype(BF16)

    def frame_cols_all(rr, carry):
        for t in range(frames_n):
            frame_cols(t, rr)
        return carry

    lax.fori_loop(1, rows_n + 1, frame_cols_all, 0)
    second = small_batch(0, first)
    for c in g_batch[0]:
        c.wait_recv()
    g_rows = [[], []]

    def next_rows(part, s):
        if s > 0:
            g_rows[part][s - 1].wait_recv()
        elif part == 1:
            for c in g_batch[1]:
                c.wait_recv()
        if s < hi_bits:
            g_rows[part].append(gather_rows(part, s))

    next_rows(0, 0)
    f_up.wait_recv()
    f_down.wait_recv()
    for t in range(frames_n):
        fr[t, 0] = fhalo_r[0, t].astype(F32) * has_up
        fr[t, rows_n + 1] = fhalo_r[1, t].astype(F32) * has_down
        frame_cols(t, 0)
        frame_cols(t, rows_n + 1)
    next_rows(1, 0)

    def frame_pixels(t):
        def one(rr, carry):
            parts = [
                xt[t, WIDE : WIDE + FEAT, pl.ds(pl.multiple_of((rr + a) * WID, WID), WID)].astype(F32)
                for a in range(3)
            ]
            parts.append(jnp.zeros((FPAD - 9 * CIN, WID), F32))
            gpre[t, pl.ds(pl.multiple_of(rr * WID, WID), WID), 0:FPAD] = (
                jnp.concatenate(parts, axis=0).T.astype(BF16)
            )
            return carry

        lax.fori_loop(0, rows_n, one, 0)

    frame_pixels(0)
    for s in range(1, hi_bits + 1):
        next_rows(0, s)
        if s <= hi_bits:
            next_rows(1, s)
        if s < frames_n:
            frame_pixels(s)
    for t in range(hi_bits + 1, frames_n):
        frame_pixels(t)

    small = small_done(0, second)
    consts[...] = small
    peep = [consts[i : i + 1, :] for i in range(3)]
    bias = [consts[4 + i : 5 + i, :] for i in range(4)]

    def cat_wt(lo, up):
        v = wt[(slice(None),) * (2 + hi_bits) + (pl.ds(lo, up - lo),)]
        return v.reshape(GATES, up - lo)

    wft[...] = cat_wt(HALL, KALL).astype(F32).T.astype(BF16)

    sub_iota = lax.broadcasted_iota(jnp.int32, (SUB, HID), 0)

    def live_cols(rr):
        return jnp.where(row0 + rr < crop_h, crop_w, 0)

    def place_state(t, v, at):
        three = [row_shift(v, -1), v, row_shift(v, 1)]
        for j in range(3):
            sc[t, at, :, j * HID : (j + 1) * HID] = three[j].astype(BF16)
        vt = v.T
        three = [lane_shift(vt, -1), vt, lane_shift(vt, 1)]
        for j in range(3):
            xt[t + 1, j * HID : (j + 1) * HID, pl.ds(pl.multiple_of(at * WID, WID), WID)] = three[j].astype(BF16)

    def forward_row(t, rr):
        limit = live_cols(rr)
        for j in range(WID // SUB):
            sl = pl.ds(pl.multiple_of(rr * WID + j * SUB, SUB), SUB)
            live = sub_iota + j * SUB < limit
            zi = gates[t, sl, 0:HID] + bias[0]
            zc = gates[t, sl, 2 * HID : 3 * HID] + bias[2]
            zo = gates[t, sl, 3 * HID :] + bias[3]
            if t > 0:
                prev = cells[t - 1, sl, :]
                zf = gates[t, sl, HID : 2 * HID] + bias[1] + peep[1] * prev
                zi = zi + peep[0] * prev
                gf = sigmoid(zf)
                gates[t, sl, HID : 2 * HID] = gf
            gi = sigmoid(zi)
            gc = jnp.tanh(zc)
            c = gi * gc
            if t > 0:
                c = c + gf * prev
            c = jnp.where(live, c, 0.0)
            go = sigmoid(zo + peep[2] * c)
            gates[t, sl, 0:HID] = gi
            gates[t, sl, 2 * HID : 3 * HID] = gc
            gates[t, sl, 3 * HID :] = go
            cells[t, sl, :] = c
            srow[j * SUB : (j + 1) * SUB, :] = jnp.where(live, go * jnp.tanh(c), 0.0)
        if t < frames_n - 1:
            place_state(t, srow[...], rr + 1)
        else:
            hlast[pl.ds(rr, 1)] = srow[...].astype(BF16)[None]

    CH = 4

    def forward_chunk(t, m):
        px = pl.ds(pl.multiple_of(m * CH * WID, CH * WID), CH * WID)
        xf = gpre[t, px, 0:FPAD]
        if t > 0:
            parts = [
                sc[t - 1, pl.ds(m * CH + a, CH)].reshape(CH * WID, WIDE) for a in range(3)
            ]
            x = jnp.concatenate(parts + [xf], axis=1)
            gates[t, px, :] = mm(x, cat_wt(0, KALL), NT)
        else:
            gates[t, px, :] = mm(xf, cat_wt(HALL, KALL), NT)

        def one(i, carry):
            forward_row(t, m * CH + i)
            return carry

        lax.fori_loop(0, CH, one, 0)

    nchunk = rows_n // CH
    hid_copies = []
    halo = None
    for t in range(frames_n):
        lax.fori_loop(1, nchunk - 1, lambda m, c: (forward_chunk(t, m), c)[1], 0)
        if halo is not None:
            halo[0].wait_recv()
            halo[1].wait_recv()
            place_state(t - 1, shalo_r[t - 1, 0].astype(F32) * has_up, 0)
            place_state(t - 1, shalo_r[t - 1, 1].astype(F32) * has_down, rows_n + 1)
        lax.fori_loop(0, 2, lambda m, c: (forward_chunk(t, m * (nchunk - 1)), c)[1], 0)
        if t < frames_n - 1:
            mid = pl.ds(HID, HID)
            halo = (
                remote(sc.at[t, 1, :, mid], shalo_r.at[t, 1], at_b, up_r),
                remote(sc.at[t, rows_n, :, mid], shalo_r.at[t, 0], at_b, down_r),
            )
            c = pltpu.make_async_copy(sc.at[t, pl.ds(1, rows_n), :, mid], hid_hbm.at[0, t], lsems.at[1 + t])
        else:
            c = pltpu.make_async_copy(hlast, hid_hbm.at[0, t], lsems.at[1 + t])
        c.start()
        hid_copies.append(c)

    cot_copy.wait()
    sums[...] = jnp.zeros_like(sums)

    def fold(v):
        return jnp.sum(v.reshape(SUB // 8, 8, HID), axis=0)

    def backward_row(t, rr):
        limit = live_cols(rr)
        parts = [None] * 7
        for j in range(WID // SUB):
            sl = pl.ds(pl.multiple_of(rr * WID + j * SUB, SUB), SUB)
            live = sub_iota + j * SUB < limit
            gi = gates[t, sl, 0:HID]
            gc = gates[t, sl, 2 * HID : 3 * HID]
            go = gates[t, sl, 3 * HID :]
            c = cells[t, sl, :]
            sq = jnp.tanh(c)
            total = cot[t, rr, j * SUB : (j + 1) * SUB, :].astype(F32)
            if t < frames_n - 1:
                total = total + gs[rr + 1, j * SUB : (j + 1) * SUB, :]
            total = jnp.where(live, total, 0.0)
            tgo = total * go
            d_out = tgo * sq * (1.0 - go)
            nxt = tgo * (1.0 - sq * sq) + peep[2] * d_out
            if t < frames_n - 1:
                nxt = nxt + gcell[sl, :]
            kept = jnp.where(live, nxt, 0.0)
            kgi = kept * gi
            d_in = kgi * gc * (1.0 - gi)
            d_cand = kgi * (1.0 - gc * gc)
            vals = [d_in, None, d_cand, d_out, None, None, d_out * c]
            if t > 0:
                gf = gates[t, sl, HID : 2 * HID]
                prev = cells[t - 1, sl, :]
                kgf = kept * gf
                d_for = kgf * prev * (1.0 - gf)
                gcell[sl, :] = kgf + peep[0] * d_in + peep[1] * d_for
                vals[1] = d_for
                vals[4] = d_in * prev
                vals[5] = d_for * prev
            gpre[t, sl, 0:HID] = d_in.astype(BF16)
            gpre[t, sl, HID : 2 * HID] = (vals[1] if t > 0 else jnp.zeros_like(d_in)).astype(BF16)
            gpre[t, sl, 2 * HID : 3 * HID] = d_cand.astype(BF16)
            gpre[t, sl, 3 * HID :] = d_out.astype(BF16)
            for i in range(7):
                if vals[i] is not None:
                    f = fold(vals[i])
                    parts[i] = f if parts[i] is None else parts[i] + f
        for i in range(7):
            if parts[i] is not None:
                sums[i] = sums[i] + parts[i]

    def state_chunk(t, m):
        px = pl.ds(pl.multiple_of(m * CH * WID, CH * WID), CH * WID)
        ybuf[...] = mm(gpre[t, px, :], cat_wt(0, HALL), NN)

        def one(i, carry):
            sl = pl.ds(pl.multiple_of(i * WID, WID), WID)
            for a in range(3):
                z = ybuf[sl, a * WIDE + HID : a * WIDE + 2 * HID]
                z = z + row_shift(ybuf[sl, a * WIDE : a * WIDE + HID], 1)
                z = z + row_shift(ybuf[sl, a * WIDE + 2 * HID : (a + 1) * WIDE], -1)
                at = m * CH + i + a
                gs[at] = gs[at] + z
            return carry

        lax.fori_loop(0, CH, one, 0)

    halo = None
    for t in reversed(range(frames_n)):
        lax.fori_loop(1, rows_n - 1, lambda rr, c: (backward_row(t, rr), c)[1], 0)
        if halo is not None:
            halo[0].wait_recv()
            halo[1].wait_recv()
            gs[1] = gs[1] + ghalo_r[t, 0].astype(F32) * has_up
            gs[rows_n] = gs[rows_n] + ghalo_r[t, 1].astype(F32) * has_down
        lax.fori_loop(0, 2, lambda k, c: (backward_row(t, k * (rows_n - 1)), c)[1], 0)
        if t > 0:
            gs[...] = jnp.zeros_like(gs)
            lax.fori_loop(0, 2, lambda k, c: (state_chunk(t, k * (nchunk - 1)), c)[1], 0)
            ghalo_s[t - 1, 0] = gs[0].astype(BF16)
            ghalo_s[t - 1, 1] = gs[rows_n + 1].astype(BF16)
            halo = (
                remote(ghalo_s.at[t - 1, 0], ghalo_r.at[t - 1, 1], at_b, up_r),
                remote(ghalo_s.at[t - 1, 1], ghalo_r.at[t - 1, 0], at_b, down_r),
            )
            lax.fori_loop(1, nchunk - 1, lambda m, c: (state_chunk(t, m), c)[1], 0)

    for i in range(7):
        at = (4 + i) if i < 4 else i - 4
        sm1[1, at_r, at : at + 1, :] = jnp.sum(sums[i], axis=0, keepdims=True)
    sm1[1, at_r, 3:4, :] = jnp.zeros((1, HID), F32)
    first = small_rows(1)

    widths = [WIDE, WIDE, WIDE, FPAD]
    stage = [0] * 4
    flight = [None] * 4
    full = (slice(None),)

    def reduce_step(q):
        s = stage[q]
        ref = acc[q]
        if s > 0 and s <= hi_bits:
            flight[q].wait_recv()
            mine = (full * s) + (hi[hi_bits - s],)
            recv = stage_recv[q * hi_bits + s - 1]
            keep = ref[s - 1][full * (1 + hi_bits - s) + (hi[hi_bits - s],)]
            ref[s][...] = keep + recv[...].astype(F32)
            del mine
        if s < hi_bits:
            away = 1 - hi[hi_bits - 1 - s]
            snd = stage_send[q * hi_bits + s]
            snd[...] = ref[s][full * (hi_bits - s) + (away,)].astype(BF16)
            flight[q] = remote(snd, stage_recv[q * hi_bits + s], at_b, partner(lo_bits + s))
        elif s == hi_bits:
            snd = last_send[q]
            snd[...] = ref[s][...].astype(BF16)
            flight[q] = [
                remote(snd.at[lax.rem(at_b + k, nbat)], last_recv[q].at[k], lax.rem(at_b + k, nbat), at_r)
                for k in range(1, nbat)
            ]
        elif s == hi_bits + 1:
            for c in flight[q]:
                c.wait_recv()
            total = ref[hi_bits][at_b]
            for k in range(1, nbat):
                total = total + last_recv[q][k].astype(F32)
            if q < 3:
                for j in range(3):
                    tap = 3 * q + j
                    at = tap * (CIN + HID) + CIN
                    nat[:, at : at + HID] = total[:, j * HID : (j + 1) * HID]
            else:
                for tap in range(9):
                    at = tap * (CIN + HID)
                    nat[:, at : at + CIN] = total[:, tap * CIN : (tap + 1) * CIN]
        stage[q] = s + 1

    facc[...] = jnp.zeros_like(facc)
    g0 = [xt[0, WIDE : WIDE + FEAT, a * WID : a * WID + pix] for a in range(3)]
    facc[0 : 9 * CIN, :] = mm(jnp.concatenate(g0, axis=0), gpre[0], NN)

    second = None
    for a in range(3):
        total = None
        for t in range(1, frames_n):
            part = mm(xt[t, :, a * WID : a * WID + pix], gpre[t], NN)
            total = part if total is None else total + part
        facc[a * FEAT : (a + 1) * FEAT, :] = facc[a * FEAT : (a + 1) * FEAT, :] + total[WIDE:, :]
        acc[a][0][...] = total[:WIDE, :].T.reshape(acc[a][0].shape)
        for q in range(a):
            reduce_step(q)
        reduce_step(a)
        if a == 0:
            second = small_batch(1, first)
    acc[3][0][...] = facc[...].T.reshape(acc[3][0].shape)
    for q in range(4):
        reduce_step(q)

    def frame_back(t):
        fgb[t] = jnp.zeros(fgb.shape[1:], F32)

        def chunk(m, carry):
            px = pl.ds(pl.multiple_of(m * CH * WID, CH * WID), CH * WID)
            y = mm(wft[0 : 9 * CIN, :], gpre[t, px, :], NT)
            for i in range(CH):
                for a in range(3):
                    part = y[a * FEAT : (a + 1) * FEAT, i * WID : (i + 1) * WID]
                    z = part[CIN : 2 * CIN]
                    z = z + lane_shift(part[0:CIN], 1)
                    z = z + lane_shift(part[2 * CIN :], -1)
                    at = m * CH + i + a
                    fgb[t, at] = fgb[t, at] + z
            return carry

        lax.fori_loop(0, nchunk, chunk, 0)
        bhalo_s[0, t] = fgb[t, 0].astype(BF16)
        bhalo_s[1, t] = fgb[t, rows_n + 1].astype(BF16)

    for t in range(frames_n):
        frame_back(t)
        for q in range(4):
            if stage[q] < hi_bits + 2 and t < frames_n - 1:
                reduce_step(q)
    f_up = remote(bhalo_s.at[0], bhalo_r.at[1], at_b, up_r)
    f_down = remote(bhalo_s.at[1], bhalo_r.at[0], at_b, down_r)
    while any(s < hi_bits + 2 for s in stage):
        for q in range(4):
            if stage[q] < hi_bits + 2:
                reduce_step(q)
    for s in range(lo_bits):
        lo_send[s][...] = nat[...].astype(BF16)
        c = remote(lo_send[s], lo_recv[s], at_b, partner(s))
        c.wait_recv()
        nat[...] = nat[...] + lo_recv[s][...].astype(F32)

    g = nat[:, 0:KROWS]
    rows_own = GATES // (nbat * nrow)
    squares = g * g
    if lo_bits:
        base = lax.rem(at_r, 1 << lo_bits) * rows_own
        ri = lax.broadcasted_iota(jnp.int32, squares.shape, 0)
        squares = jnp.where((ri >= base) & (ri < base + rows_own), squares, 0.0)
    sm1[2, at_r] = jnp.broadcast_to(jnp.sum(squares), (8, HID))
    third = small_rows(2)
    grad_ref[...] = g
    small = small_done(1, second)
    small_out[...] = small
    f_up.wait_recv()
    f_down.wait_recv()
    fourth = small_batch(2, third)
    for t in range(frames_n):
        fgb[t, 1] = fgb[t, 1] + bhalo_r[0, t].astype(F32) * has_up
        fgb[t, rows_n] = fgb[t, rows_n] + bhalo_r[1, t].astype(F32) * has_down
        fg_ref[0, t] = jnp.where(live3, jnp.swapaxes(fgb[t, 1 : rows_n + 1], 0, 1), 0.0)
    squares = small_done(2, fourth) + jnp.sum(small * small)
    norm_out[...] = jnp.sqrt(squares)

    for c in hid_copies:
        c.wait()
    for c in pending:
        c.wait_send()
    del lane


def adamw_update(weight, gradient, first, second, scale):
    clipped = gradient * scale
    first_new = BETA_ONE * first + (1.0 - BETA_ONE) * clipped
    second_new = BETA_TWO * second + (1.0 - BETA_TWO) * clipped * clipped
    first_hat = first_new / (1.0 - BETA_ONE**STEP)
    second_hat = second_new / (1.0 - BETA_TWO**STEP)
    weight_new = weight - LEARN_RATE * (
        first_hat / (jnp.sqrt(second_hat) + ADAM_EPS) + WEIGHT_DECAY * weight
    )
    return (weight_new, first_new, second_new)


def local(
    nbat,
    nrow,
    frames,
    crop_sizes,
    kernel,
    gate_bias,
    peepholes,
    cotangent,
    kernel_first,
    kernel_second,
    bias_first,
    bias_second,
    peep_first,
    peep_second,
):
    frames_n, rows_n = frames.shape[1], frames.shape[3]
    pix = rows_n * WID
    own = kernel.shape[1]
    share = max(1, UNIT // own)
    lo_bits = int(math.log2(share))
    hi_bits = int(math.log2(nrow)) - lo_bits
    at_b = lax.axis_index("batch")
    at_r = lax.axis_index("rows")
    flat = (at_b * nrow + at_r) * own
    pw = peepholes.shape[1]

    kt = kernel.T
    if lo_bits:
        kt = lax.dynamic_update_slice(
            jnp.zeros((UNIT, KROWS), F32), kt, (lax.rem(at_r, share) * own, 0)
        )
    bias_tile = lax.dynamic_update_slice(jnp.zeros((GATES,), F32), gate_bias, (flat,)).reshape(4, HID)
    peep_mine = jnp.where(at_r == 0, peepholes, 0.0)
    peep_tile = lax.dynamic_update_slice(jnp.zeros((4, HID), F32), peep_mine, (0, at_b * pw))
    small = jnp.concatenate([peep_tile, bias_tile], axis=0)

    blocks = (nbat,) + (2,) * hi_bits
    widths = [WIDE, WIDE, WIDE, FPAD]
    vm = functools.partial(pltpu.VMEM)
    stage_shapes = []
    for wide in widths:
        for s in range(hi_bits):
            stage_shapes.append(vm((nbat,) + (2,) * (hi_bits - s - 1) + (UNIT, wide), BF16))
    last_shapes = [vm((nbat, UNIT, wide), BF16) for wide in widths]
    acc_shapes = []
    for wide in widths:
        acc_shapes.append([vm((nbat,) + (2,) * (hi_bits - s) + (UNIT, wide), F32) for s in range(hi_bits + 1)])
    ncopies = (
        3 * (nrow - 1 + nbat - 1)
        + 2 * (nbat - 1 + hi_bits)
        + 4 * (hi_bits + nbat - 1)
        + 4
        + 4 * (frames_n - 1)
        + 2 * lo_bits
    )
    scratch = [
        vm(blocks + (UNIT, KALL), BF16),
        vm((FPAD, GATES), BF16),
        vm((frames_n, rows_n + 2, CIN, WID), F32),
        vm((frames_n, WIDE + FEAT, (rows_n + 2) * WID), BF16),
        vm((frames_n - 1, rows_n + 2, WID, WIDE), BF16),
        vm((frames_n, pix, GATES), F32),
        vm((frames_n, pix, HID), F32),
        vm((frames_n, pix, GATES), BF16),
        vm((pix, HID), F32),
        vm((rows_n + 2, WID, HID), F32),
        vm((4 * WID, HALL), F32),
        vm((frames_n, rows_n + 2, CIN, WID), F32),
        vm((frames_n, rows_n, WID, HID), BF16),
        vm((rows_n, WID, HID), BF16),
        vm((WID, HID), F32),
        vm((8, HID), F32),
        vm((7, 8, HID), F32),
        acc_shapes,
        vm((FPAD, GATES), F32),
        vm((2, frames_n, CIN, WID), BF16),
        vm((2, frames_n, CIN, WID), BF16),
        vm((frames_n - 1, 2, WID, HID), BF16),
        vm((frames_n - 1, 2, WID, HID), BF16),
        vm((frames_n - 1, 2, WID, HID), BF16),
        vm((2, frames_n, CIN, WID), BF16),
        vm((2, frames_n, CIN, WID), BF16),
        vm((UNIT, KALL), F32),
        vm((3, nrow, 8, HID), F32),
        vm((3, nbat, 8, HID), F32),
    ]
    scratch += stage_shapes + stage_shapes + last_shapes + last_shapes
    scratch += [vm((UNIT, KALL), BF16)] * (3 * lo_bits)
    scratch += [
        pltpu.SemaphoreType.DMA((ncopies,)),
        pltpu.SemaphoreType.DMA((ncopies,)),
        pltpu.SemaphoreType.DMA((1 + frames_n,)),
    ]
    smem = pl.BlockSpec(memory_space=pltpu.SMEM)
    vmem = pl.BlockSpec(memory_space=pltpu.VMEM)
    hbm = pl.BlockSpec(memory_space=pl.ANY)
    dims = (nbat, nrow, frames_n, rows_n, hi_bits, lo_bits)
    hidden_seq, frames_grad, kernel_sum, small_sum, norm = pl.pallas_call(
        functools.partial(layer_kernel, dims),
        out_shape=(
            jax.ShapeDtypeStruct(cotangent.shape, BF16),
            jax.ShapeDtypeStruct(frames.shape, F32),
            jax.ShapeDtypeStruct((UNIT, KROWS), F32),
            jax.ShapeDtypeStruct((8, HID), F32),
            jax.ShapeDtypeStruct((8, HID), F32),
        ),
        in_specs=[smem, vmem, vmem, vmem, hbm],
        out_specs=(hbm, vmem, vmem, vmem, vmem),
        scratch_shapes=scratch,
        compiler_params=pltpu.CompilerParams(
            collective_id=0, has_side_effects=True, vmem_limit_bytes=63 << 20
        ),
        name="layer",
    )(crop_sizes, frames, kt, small, cotangent)

    if lo_bits:
        kernel_sum = lax.dynamic_slice_in_dim(kernel_sum, lax.rem(at_r, share) * own, own, 0)
    grad_norm = norm[0, 0]
    scale = jnp.minimum(1.0, CLIP_AT / (grad_norm + 1e-06))
    kernel_grad = kernel_sum.T
    bias_grad = lax.dynamic_slice(small_sum[4:8].reshape(GATES), (flat,), (own,))
    peep_grad = lax.dynamic_slice(small_sum, (0, at_b * pw), (3, pw))
    kernel_new, kernel_first_new, kernel_second_new = adamw_update(
        kernel, kernel_grad, kernel_first, kernel_second, scale
    )
    bias_new, bias_first_new, bias_second_new = adamw_update(
        gate_bias, bias_grad, bias_first, bias_second, scale
    )
    peep_new, peep_first_new, peep_second_new = adamw_update(
        peepholes, peep_grad, peep_first, peep_second, scale
    )
    return (
        hidden_seq,
        frames_grad,
        grad_norm,
        kernel_new,
        kernel_first_new,
        kernel_second_new,
        bias_new,
        bias_first_new,
        bias_second_new,
        peep_new,
        peep_first_new,
        peep_second_new,
    )


def solution(mesh):
    return jax.shard_map(
        functools.partial(local, mesh.shape["batch"], mesh.shape["rows"]),
        mesh=mesh,
        in_specs=(
            P("batch", None, None, "rows", None),
            P("batch", None),
            P(None, ("batch", "rows")),
            P(("batch", "rows")),
            P(None, "batch"),
            P("batch", None, "rows", None, None),
            P(None, ("batch", "rows")),
            P(None, ("batch", "rows")),
            P(("batch", "rows")),
            P(("batch", "rows")),
            P(None, "batch"),
            P(None, "batch"),
        ),
        out_specs=(
            P("batch", None, "rows", None, None),
            P("batch", None, None, "rows", None),
            P(),
            P(None, ("batch", "rows")),
            P(None, ("batch", "rows")),
            P(None, ("batch", "rows")),
            P(("batch", "rows")),
            P(("batch", "rows")),
            P(("batch", "rows")),
            P(None, "batch"),
            P(None, "batch"),
            P(None, "batch"),
        ),
        check_vma=False,
    )
```

```python
import functools

import jax
import jax.numpy as jnp
from jax import lax
from jax.experimental import pallas as pl
from jax.experimental.pallas import tpu as pltpu
from jax.sharding import PartitionSpec as P

CIN = 16
HID = 128
GATES = 512
KROWS = 1296
WID = 128
STEP = 5
CLIP_AT = 0.02
LEARN_RATE = 0.02
BETA_ONE = 0.9
BETA_TWO = 0.999
WEIGHT_DECAY = 0.01
ADAM_EPS = 1e-08

F32 = jnp.float32
BF16 = jnp.bfloat16
MESH = pl.DeviceIdType.MESH
NT = (((1,), (1,)), ((), ()))
NN = (((1,), (0,)), ((), ()))

WIDE = 3 * HID
HALL = 3 * WIDE
FEAT = 3 * CIN
FPAD = 256
KALL = HALL + FPAD
PART = 512
SUB = 32
UNIT = 16


def sigmoid(v):
    return 0.5 * jnp.tanh(0.5 * v) + 0.5


def mm(a, b, dims):
    return lax.dot_general(a, b, dims, preferred_element_type=F32)


def layer_kernel(
    dims,
    crop_ref,
    frames_ref,
    kt_ref,
    bias_ref,
    peep_ref,
    cot_hbm,
    hid_hbm,
    fg_hbm,
    grad_ref,
    small_out,
    norm_out,
    wt,
    wft,
    fr,
    xt,
    sc,
    gates,
    cells,
    gpre,
    gs,
    cot,
    srow,
    consts,
    sums,
    acc,
    fzero,
    fgo,
    fhalo_s,
    fhalo_r,
    shalo_r,
    ghalo_s,
    ghalo_r,
    bhalo_s,
    bhalo_r,
    nat,
    *rest,
):
    nbat, nrow, frames_n, rows_n, nfar, nmid, ncore, nlow = dims
    pix = rows_n * WID
    rest = list(rest)
    core_send, core_recv, mid_send, mid_recv, far_send, far_recv = (
        [rest.pop(0) for _ in range(3)] for _ in range(6)
    )
    small_bufs = [rest.pop(0) for _ in range(4)]
    low_send, low_recv = rest.pop(0), rest.pop(0)
    sems = rest.pop(0)
    rsems = rest.pop(0)
    lsems = rest.pop(0)

    at_b = lax.axis_index("batch")
    at_r = lax.axis_index("rows")
    counter = [0]
    pending = []

    def remote(src, dst, bat, row):
        i = counter[0]
        counter[0] += 1
        c = pltpu.make_async_remote_copy(
            src_ref=src, dst_ref=dst, send_sem=sems.at[i], recv_sem=rsems.at[i],
            device_id=(bat, row), device_id_type=MESH,
        )
        c.start()
        pending.append(c)
        return c

    far, near = at_b // 2, at_b % 2
    low = at_r % nlow
    core = (at_r // nlow) % ncore
    half = nmid // 2
    mid = near * half + at_r // (nlow * ncore)

    def device(f, m, c, w):
        return (f * 2 + m // half, ((m % half) * ncore + c) * nlow + w)

    def far_peer(k):
        return device(lax.rem(far + k, nfar), mid, core, low)

    def mid_peer(k):
        return device(far, lax.rem(mid + k, nmid), core, low)

    def core_peer(k):
        return device(far, mid, lax.rem(core + k, ncore), low)

    def low_peer(k):
        return device(far, mid, core, lax.rem(low + k, nlow))

    groups = [(nfar, far_peer, far), (nmid, mid_peer, mid), (ncore, core_peer, core), (nlow, low_peer, low)]
    up_r = lax.rem(at_r + nrow - 1, nrow)
    down_r = lax.rem(at_r + 1, nrow)

    barrier = pltpu.get_barrier_semaphore()
    greeted = 2
    pl.semaphore_signal(barrier, inc=1, device_id=(at_b, up_r), device_id_type=MESH)
    pl.semaphore_signal(barrier, inc=1, device_id=(at_b, down_r), device_id_type=MESH)
    for size, peer, _ in groups:
        for k in range(1, size):
            pl.semaphore_signal(barrier, inc=1, device_id=peer(k), device_id_type=MESH)
            greeted += 1

    cot_copy = pltpu.make_async_copy(cot_hbm.at[0], cot, lsems.at[0])
    cot_copy.start()

    ktv = kt_ref[...]
    own = []
    for tap in range(9):
        own.append(ktv[:, tap * (CIN + HID) + CIN : (tap + 1) * (CIN + HID)])
    for tap in range(9):
        own.append(ktv[:, tap * (CIN + HID) : tap * (CIN + HID) + CIN])
    own.append(jnp.zeros((UNIT, FPAD - 9 * CIN), F32))
    wt[far, mid, core] = jnp.concatenate(own, axis=1).astype(BF16)

    rows_own = GATES // (nbat * nrow)
    flat = (at_b * nrow + at_r) * rows_own
    peep_own = HID // nbat
    tile_row = lax.broadcasted_iota(jnp.int32, (8, HID), 0)
    consts[...] = jnp.zeros_like(consts)
    consts[0:3, 0:peep_own] = peep_ref[...]
    consts[4:5, 0:rows_own] = bias_ref[...]
    peep_tile = pltpu.roll(jnp.where(tile_row < 3, consts[...], 0.0), at_b * peep_own, 1)
    bias_tile = pltpu.roll(jnp.broadcast_to(consts[4:5, :], (8, HID)), flat % HID, 1)
    bias_tile = jnp.where(tile_row == 4 + flat // HID, bias_tile, 0.0)
    start_tile = jnp.where(at_r == 0, peep_tile, 0.0) + bias_tile

    small_step = [0] * 3
    small_sum = [None] * 3
    small_moving = [None] * 3

    def small_next(i, tile=None):
        s = small_step[i]
        small_step[i] = s + 1
        while s < 4 and groups[s][0] == 1:
            s += 1
            small_step[i] = s + 1
        if tile is None:
            done = s - 1
            while groups[done][0] == 1:
                done -= 1
            for c in small_moving[i]:
                c.wait_recv()
            tile = small_bufs[done][i, 0]
            for k in range(1, groups[done][0]):
                tile = tile + small_bufs[done][i, k]
        if s < 4:
            size, peer, place = groups[s]
            ref = small_bufs[s].at[i, place]
            ref[...] = tile
            small_moving[i] = [remote(ref, ref, *peer(k)) for k in range(1, size)]
            return None
        return tile

    def small_finish(i):
        while True:
            tile = small_next(i)
            if tile is not None:
                return tile

    lanes = [(HALL, KALL), (0, WIDE), (WIDE, 2 * WIDE), (2 * WIDE, HALL)]
    steps = [0] * 4
    moving = [None] * 4

    def gather_low():
        if nlow > 1:
            low_send[...] = wt[far, mid, core]
            copies = [remote(low_send, low_recv.at[0, k - 1], *low_peer(k)) for k in range(1, nlow)]
            total = low_send[...]
            for k in range(1, nlow):
                copies[k - 1].wait_recv()
                total = total + low_recv[0, k - 1]
            wt[far, mid, core] = total

    def gather_step(i):
        lo, up = lanes[i]
        cols = pl.ds(lo, up - lo)
        s = steps[i]
        steps[i] = s + 1
        if 0 < s < 4:
            for c in moving[i]:
                c.wait_recv()
        if s < 3:
            size, peer, _ = groups[s]
            if s == 0:
                ref = wt.at[far, mid, core, :, cols]
            elif s == 1:
                ref = wt.at[:, mid, core, :, cols]
            else:
                ref = wt.at[:, :, core, :, cols]
            moving[i] = [remote(ref, ref, *peer(k)) for k in range(1, size)]

    crop_h = crop_ref[0, 0]
    crop_w = crop_ref[0, 1]
    row0 = at_r * rows_n
    has_up = (at_r > 0).astype(F32)
    has_down = (at_r < nrow - 1).astype(F32)

    rr3 = lax.broadcasted_iota(jnp.int32, (CIN, rows_n, WID), 1) + row0
    cc3 = lax.broadcasted_iota(jnp.int32, (CIN, rows_n, WID), 2)
    live3 = (rr3 < crop_h) & (cc3 < crop_w)
    for t in range(frames_n):
        masked = jnp.where(live3, frames_ref[0, t].astype(F32), 0.0)
        fr[t, 1 : rows_n + 1] = jnp.swapaxes(masked, 0, 1)
        fhalo_s[0, t] = fr[t, 1].astype(BF16)
        fhalo_s[1, t] = fr[t, rows_n].astype(BF16)

    def lane_shift(v, by):
        at = lax.broadcasted_iota(jnp.int32, v.shape, 1)
        if by > 0:
            return jnp.where(at == WID - 1, 0.0, pltpu.roll(v, WID - 1, 1))
        return jnp.where(at == 0, 0.0, pltpu.roll(v, 1, 1))

    def row_shift(v, by):
        at = lax.broadcasted_iota(jnp.int32, v.shape, 0)
        if by > 0:
            return jnp.where(at == WID - 1, 0.0, pltpu.roll(v, WID - 1, 0))
        return jnp.where(at == 0, 0.0, pltpu.roll(v, 1, 0))

    def frame_cols(t, rr):
        v = fr[t, rr]
        three = jnp.concatenate([lane_shift(v, -1), v, lane_shift(v, 1)], axis=0)
        xt[t, WIDE : WIDE + FEAT, pl.ds(pl.multiple_of(rr * WID, WID), WID)] = three.astype(BF16)

    def frame_cols_all(rr, carry):
        for t in range(frames_n):
            frame_cols(t, rr)
        return carry

    def frame_pixels(t, lo, up):
        def one(rr, carry):
            parts = [
                xt[t, WIDE : WIDE + FEAT, pl.ds(pl.multiple_of((rr + a) * WID, WID), WID)].astype(F32)
                for a in range(3)
            ]
            parts.append(jnp.zeros((FPAD - 9 * CIN, WID), F32))
            gpre[t, pl.ds(pl.multiple_of(rr * WID, WID), WID), 0:FPAD] = (
                jnp.concatenate(parts, axis=0).T.astype(BF16)
            )
            return carry

        lax.fori_loop(lo, up, one, 0)

    lax.fori_loop(1, rows_n + 1, frame_cols_all, 0)
    frame_pixels(0, 1, rows_n - 1)

    pl.semaphore_wait(barrier, greeted)
    gather_low()
    gather_step(0)
    small_next(0, start_tile)
    f_up = remote(fhalo_s.at[0], fhalo_r.at[1], at_b, up_r)
    f_down = remote(fhalo_s.at[1], fhalo_r.at[0], at_b, down_r)
    gather_step(1)
    gather_step(2)
    gather_step(3)
    if frames_n > 1:
        frame_pixels(1, 1, rows_n - 1)
    gather_step(0)
    small_next(0)
    f_up.wait_recv()
    f_down.wait_recv()
    for t in range(frames_n):
        fr[t, 0] = fhalo_r[0, t].astype(F32) * has_up
        fr[t, rows_n + 1] = fhalo_r[1, t].astype(F32) * has_down
        frame_cols(t, 0)
        frame_cols(t, rows_n + 1)
    for t in range(min(2, frames_n)):
        frame_pixels(t, 0, 1)
        frame_pixels(t, rows_n - 1, rows_n)
    gather_step(1)
    if frames_n > 2:
        frame_pixels(2, 0, rows_n)
    gather_step(2)
    gather_step(0)
    small_next(0)
    gather_step(3)
    for t in range(3, frames_n):
        frame_pixels(t, 0, rows_n)
    gather_step(0)

    consts[...] = small_finish(0)
    peep = [consts[i : i + 1, :] for i in range(3)]
    bias = [consts[4 + i : 5 + i, :] for i in range(4)]

    def cat_wt(lo, up):
        return wt[:, :, :, :, lo:up].reshape(GATES, up - lo)

    sub_iota = lax.broadcasted_iota(jnp.int32, (SUB, HID), 0)

    def live_cols(rr):
        return jnp.where(row0 + rr < crop_h, crop_w, 0)

    def place_state(t, v, at):
        three = [row_shift(v, -1), v, row_shift(v, 1)]
        for j in range(3):
            sc[t, at, :, j * HID : (j + 1) * HID] = three[j].astype(BF16)
        vt = v.T
        three = [lane_shift(vt, -1), vt, lane_shift(vt, 1)]
        for j in range(3):
            xt[t + 1, j * HID : (j + 1) * HID, pl.ds(pl.multiple_of(at * WID, WID), WID)] = three[j].astype(BF16)

    def forward_row(t, rr):
        limit = live_cols(rr)
        for j in range(WID // SUB):
            sl = pl.ds(pl.multiple_of(rr * WID + j * SUB, SUB), SUB)
            live = sub_iota + j * SUB < limit
            zi = gates[t, sl, 0:HID] + bias[0]
            zc = gates[t, sl, 2 * HID : 3 * HID] + bias[2]
            zo = gates[t, sl, 3 * HID :] + bias[3]
            if t > 0:
                prev = cells[t - 1, sl, :]
                zf = gates[t, sl, HID : 2 * HID] + bias[1] + peep[1] * prev
                zi = zi + peep[0] * prev
                gf = sigmoid(zf)
                gates[t, sl, HID : 2 * HID] = gf
            gi = sigmoid(zi)
            gc = jnp.tanh(zc)
            c = gi * gc
            if t > 0:
                c = c + gf * prev
            c = jnp.where(live, c, 0.0)
            go = sigmoid(zo + peep[2] * c)
            gates[t, sl, 0:HID] = gi
            gates[t, sl, 2 * HID : 3 * HID] = gc
            gates[t, sl, 3 * HID :] = go
            cells[t, sl, :] = c
            srow[j * SUB : (j + 1) * SUB, :] = jnp.where(live, go * jnp.tanh(c), 0.0)
        if t < frames_n - 1:
            place_state(t, srow[...], rr + 1)
        else:
            sc[0, rr + 1, :, 0:HID] = srow[...].astype(BF16)

    CH = 4

    def forward_chunk(t, m):
        px = pl.ds(pl.multiple_of(m * CH * WID, CH * WID), CH * WID)
        xf = gpre[t, px, 0:FPAD]
        if t > 0:
            parts = [
                sc[t - 1, pl.ds(m * CH + a, CH)].reshape(CH * WID, WIDE) for a in range(3)
            ]
            x = jnp.concatenate(parts + [xf], axis=1)
            gates[t, px, :] = mm(x, cat_wt(0, KALL), NT)
        else:
            gates[t, px, :] = mm(xf, cat_wt(HALL, KALL), NT)

        def one(i, carry):
            forward_row(t, m * CH + i)
            return carry

        lax.fori_loop(0, CH, one, 0)

    nchunk = rows_n // CH
    hid_copies = []
    halo = None
    for t in range(frames_n):
        if t == 0:
            for m in range(nchunk):
                forward_chunk(0, m)
                if m < 3:
                    gather_step(1 + m)
            for i in range(1, 4):
                while steps[i] < 4:
                    gather_step(i)
        else:
            lax.fori_loop(1, nchunk - 1, lambda m, c: (forward_chunk(t, m), c)[1], 0)
        if halo is not None:
            halo[0].wait_recv()
            halo[1].wait_recv()
            place_state(t - 1, shalo_r[t - 1, 0].astype(F32) * has_up, 0)
            place_state(t - 1, shalo_r[t - 1, 1].astype(F32) * has_down, rows_n + 1)
        if t > 0:
            lax.fori_loop(0, 2, lambda m, c: (forward_chunk(t, m * (nchunk - 1)), c)[1], 0)
        if t < frames_n - 1:
            center = pl.ds(HID, HID)
            halo = (
                remote(sc.at[t, 1, :, center], shalo_r.at[t, 1], at_b, up_r),
                remote(sc.at[t, rows_n, :, center], shalo_r.at[t, 0], at_b, down_r),
            )
            c = pltpu.make_async_copy(sc.at[t, pl.ds(1, rows_n), :, center], hid_hbm.at[0, t], lsems.at[1 + t])
        else:
            c = pltpu.make_async_copy(
                sc.at[0, pl.ds(1, rows_n), :, pl.ds(0, HID)], hid_hbm.at[0, t], lsems.at[1 + t]
            )
        c.start()
        hid_copies.append(c)

    cot_copy.wait()
    sums[...] = jnp.zeros_like(sums)

    def fold(v):
        return jnp.sum(v.reshape(SUB // 8, 8, HID), axis=0)

    def backward_row(t, rr):
        limit = live_cols(rr)
        parts = [None] * 7
        for j in range(WID // SUB):
            sl = pl.ds(pl.multiple_of(rr * WID + j * SUB, SUB), SUB)
            live = sub_iota + j * SUB < limit
            gi = gates[t, sl, 0:HID]
            gc = gates[t, sl, 2 * HID : 3 * HID]
            go = gates[t, sl, 3 * HID :]
            c = cells[t, sl, :]
            sq = jnp.tanh(c)
            total = cot[t, rr, j * SUB : (j + 1) * SUB, :].astype(F32)
            if t < frames_n - 1:
                total = total + gs[rr + 1, j * SUB : (j + 1) * SUB, :]
            total = jnp.where(live, total, 0.0)
            tgo = total * go
            d_out = tgo * sq * (1.0 - go)
            nxt = tgo * (1.0 - sq * sq) + peep[2] * d_out
            if t < frames_n - 1:
                nxt = nxt + cells[t + 1, sl, :]
            kept = jnp.where(live, nxt, 0.0)
            kgi = kept * gi
            d_in = kgi * gc * (1.0 - gi)
            d_cand = kgi * (1.0 - gc * gc)
            vals = [d_in, None, d_cand, d_out, None, None, d_out * c]
            if t > 0:
                gf = gates[t, sl, HID : 2 * HID]
                prev = cells[t - 1, sl, :]
                kgf = kept * gf
                d_for = kgf * prev * (1.0 - gf)
                cells[t, sl, :] = kgf + peep[0] * d_in + peep[1] * d_for
                vals[1] = d_for
                vals[4] = d_in * prev
                vals[5] = d_for * prev
            gpre[t, sl, 0:HID] = d_in.astype(BF16)
            gpre[t, sl, HID : 2 * HID] = (vals[1] if t > 0 else jnp.zeros_like(d_in)).astype(BF16)
            gpre[t, sl, 2 * HID : 3 * HID] = d_cand.astype(BF16)
            gpre[t, sl, 3 * HID :] = d_out.astype(BF16)
            for i in range(7):
                if vals[i] is not None:
                    f = fold(vals[i])
                    parts[i] = f if parts[i] is None else parts[i] + f
        for i in range(7):
            if parts[i] is not None:
                sums[i] = sums[i] + parts[i]

    def state_chunk(t, m):
        px = pl.ds(pl.multiple_of(m * CH * WID, CH * WID), CH * WID)
        y = mm(gpre[t, px, :], cat_wt(0, HALL), NN)
        for a in range(3):
            buf = acc[a][0]
            buf[..., 0:WIDE] = y[:, a * WIDE : (a + 1) * WIDE].reshape(buf.shape[:-1] + (WIDE,))

        def one(i, carry):
            for a in range(3):
                buf = acc[a][0]
                per = nfar // CH
                three = [
                    buf[pl.ds(i * per, per), :, :, :, j * HID : (j + 1) * HID].reshape(WID, HID)
                    for j in range(3)
                ]
                z = three[1] + row_shift(three[0], 1) + row_shift(three[2], -1)
                at = m * CH + i + a
                gs[at] = gs[at] + z
            return carry

        lax.fori_loop(0, CH, one, 0)

    halo = None
    for t in reversed(range(frames_n)):
        lax.fori_loop(1, rows_n - 1, lambda rr, c: (backward_row(t, rr), c)[1], 0)
        if halo is not None:
            halo[0].wait_recv()
            halo[1].wait_recv()
            gs[1] = gs[1] + ghalo_r[t, 0].astype(F32) * has_up
            gs[rows_n] = gs[rows_n] + ghalo_r[t, 1].astype(F32) * has_down
        lax.fori_loop(0, 2, lambda k, c: (backward_row(t, k * (rows_n - 1)), c)[1], 0)
        if t > 0:
            gs[...] = jnp.zeros_like(gs)
            lax.fori_loop(0, 2, lambda k, c: (state_chunk(t, k * (nchunk - 1)), c)[1], 0)
            ghalo_s[t - 1, 0] = gs[0].astype(BF16)
            ghalo_s[t - 1, 1] = gs[rows_n + 1].astype(BF16)
            halo = (
                remote(ghalo_s.at[t - 1, 0], ghalo_r.at[t - 1, 1], at_b, up_r),
                remote(ghalo_s.at[t - 1, 1], ghalo_r.at[t - 1, 0], at_b, down_r),
            )
            lax.fori_loop(1, nchunk - 1, lambda m, c: (state_chunk(t, m), c)[1], 0)

    rows = [jnp.sum(sums[i], axis=0, keepdims=True) for i in range(7)]
    small_next(1, jnp.concatenate(rows[4:] + [jnp.zeros((1, HID), F32)] + rows[:4], axis=0))

    stage = [0] * 3
    flight = [None] * 3
    parts = [[acc[q][0], acc[q][1] if ncore > 1 else acc[q][0].at[:, :, 0]] for q in range(3)]

    def reduce_step(q):
        s = stage[q]
        stage[q] = s + 1
        first, second = parts[q]
        if s == 0 and ncore > 1:
            core_send[q][...] = first[:, :, 1 - core].astype(BF16)
            flight[q] = [remote(core_send[q], core_recv[q], *core_peer(1))]
        elif s == 1:
            if ncore > 1:
                flight[q][0].wait_recv()
                second[...] = first[:, :, core] + core_recv[q][...].astype(F32)
            flight[q] = []
            for k in range(1, nmid):
                to = lax.rem(mid + k, nmid)
                mid_send[q][k - 1] = second[:, to].astype(BF16)
                flight[q].append(remote(mid_send[q].at[k - 1], mid_recv[q].at[k - 1], *mid_peer(k)))
        elif s == 2:
            total = second[:, mid]
            for k in range(1, nmid):
                flight[q][k - 1].wait_recv()
                total = total + mid_recv[q][k - 1].astype(F32)
            second[:, mid] = total
            far_send[q][...] = total.astype(BF16)
            flight[q] = []
            for k in range(1, nfar):
                to = lax.rem(far + k, nfar)
                flight[q].append(remote(far_send[q].at[to], far_recv[q].at[k - 1], *far_peer(k)))
        elif s == 3:
            total = second[far, mid]
            for k in range(1, nfar):
                flight[q][k - 1].wait_recv()
                total = total + far_recv[q][k - 1].astype(F32)
            for j in range(3):
                at = (3 * q + j) * (CIN + HID)
                nat[:, at : at + CIN] = total[:, WIDE + j * CIN : WIDE + (j + 1) * CIN]
                nat[:, at + CIN : at + CIN + HID] = total[:, j * HID : (j + 1) * HID]

    g0 = [xt[0, WIDE : WIDE + FEAT, a * WID : a * WID + pix] for a in range(3)]
    fzero[...] = mm(jnp.concatenate(g0, axis=0), gpre[0], NN)

    for a in range(3):
        total = None
        for t in range(1, frames_n):
            part = mm(xt[t, :, a * WID : a * WID + pix], gpre[t], NN)
            total = part if total is None else total + part
            if t == 1 and a > 0:
                if a > 1:
                    reduce_step(a - 2)
                reduce_step(a - 1)
                small_next(1)
        extra = total[WIDE:, :] + fzero[a * FEAT : (a + 1) * FEAT, :]
        whole = jnp.concatenate([total[:WIDE, :], extra, jnp.zeros((PART - WIDE - FEAT, GATES), F32)], axis=0)
        acc[a][0][...] = whole.T.reshape(acc[a][0].shape)
        reduce_step(a)

    fgb = fr

    def frame_back(t):
        fgb[t] = jnp.zeros(fgb.shape[1:], F32)

        def chunk(m, carry):
            px = pl.ds(pl.multiple_of(m * CH * WID, CH * WID), CH * WID)
            y = mm(wft[0 : 9 * CIN, :], gpre[t, px, :], NT)
            for i in range(CH):
                for a in range(3):
                    part = y[a * FEAT : (a + 1) * FEAT, i * WID : (i + 1) * WID]
                    z = part[CIN : 2 * CIN]
                    z = z + lane_shift(part[0:CIN], 1)
                    z = z + lane_shift(part[2 * CIN :], -1)
                    at = m * CH + i + a
                    fgb[t, at] = fgb[t, at] + z
            return carry

        lax.fori_loop(0, nchunk, chunk, 0)
        bhalo_s[0, t] = fgb[t, 0].astype(BF16)
        bhalo_s[1, t] = fgb[t, rows_n + 1].astype(BF16)

    wft[...] = cat_wt(HALL, KALL).astype(F32).T.astype(BF16)
    after = [[2], [1, 0], [], []]
    for t in range(frames_n):
        frame_back(t)
        for q in after[t] if t < 4 else []:
            reduce_step(q)
    f_up = remote(bhalo_s.at[0], bhalo_r.at[1], at_b, up_r)
    f_down = remote(bhalo_s.at[1], bhalo_r.at[0], at_b, down_r)
    for q in (2, 1, 0):
        while stage[q] < 3:
            reduce_step(q)
    for q in range(3):
        while stage[q] < 4:
            reduce_step(q)
    if nlow > 1:
        low_send[...] = nat[...].astype(BF16)
        copies = [remote(low_send, low_recv.at[1, k - 1], *low_peer(k)) for k in range(1, nlow)]
        total = nat[...]
        for k in range(1, nlow):
            copies[k - 1].wait_recv()
            total = total + low_recv[1, k - 1].astype(F32)
        nat[...] = total

    g = nat[:, 0:KROWS]
    squares = g * g
    if nlow > 1:
        base = low * rows_own
        ri = lax.broadcasted_iota(jnp.int32, squares.shape, 0)
        squares = jnp.where((ri >= base) & (ri < base + rows_own), squares, 0.0)
    small_next(2, jnp.broadcast_to(jnp.sum(squares), (8, HID)))
    grad_ref[...] = g
    small = small_finish(1)
    small_out[...] = small
    f_up.wait_recv()
    f_down.wait_recv()
    small_next(2)
    for t in range(frames_n):
        fgb[t, 1] = fgb[t, 1] + bhalo_r[0, t].astype(F32) * has_up
        fgb[t, rows_n] = fgb[t, rows_n] + bhalo_r[1, t].astype(F32) * has_down
        fgo[t] = jnp.where(live3, jnp.swapaxes(fgb[t, 1 : rows_n + 1], 0, 1), 0.0)
    c = pltpu.make_async_copy(fgo, fg_hbm.at[0], lsems.at[1 + frames_n])
    c.start()
    hid_copies.append(c)
    squares = small_finish(2) + jnp.sum(small * small)
    norm_out[...] = jnp.sqrt(squares)

    for c in hid_copies:
        c.wait()
    for c in pending:
        c.wait_send()


def adamw_update(weight, gradient, first, second, scale):
    clipped = gradient * scale
    first_new = BETA_ONE * first + (1.0 - BETA_ONE) * clipped
    second_new = BETA_TWO * second + (1.0 - BETA_TWO) * clipped * clipped
    first_hat = first_new / (1.0 - BETA_ONE**STEP)
    second_hat = second_new / (1.0 - BETA_TWO**STEP)
    weight_new = weight - LEARN_RATE * (
        first_hat / (jnp.sqrt(second_hat) + ADAM_EPS) + WEIGHT_DECAY * weight
    )
    return (weight_new, first_new, second_new)


def update_kernel(
    dims, hid_in, fg_in, norm_ref, sum_ref, small_ref,
    k_ref, b_ref, p_ref, k1_ref, k2_ref, b1_ref, b2_ref, p1_ref, p2_ref,
    hid_out, fg_out, norm_out, ko, k1o, k2o, bo, b1o, b2o, po, p1o, p2o, hid_buf, fg_buf, sems,
):
    nbat, nrow = dims
    frames_n = hid_buf.shape[0]
    fetch, put = [], []
    for t in range(frames_n):
        for i, (src, buf, dst) in enumerate(((hid_in, hid_buf, hid_out), (fg_in, fg_buf, fg_out))):
            fetch.append(pltpu.make_async_copy(src.at[0, t], buf.at[t], sems.at[i, t]))
            put.append(pltpu.make_async_copy(buf.at[t], dst.at[0, t], sems.at[2 + i, t]))
    for c in fetch:
        c.start()
    at_b = lax.axis_index("batch")
    at_r = lax.axis_index("rows")
    norm_out[0, 0] = norm_ref[0, 0]
    norm = jnp.full((1, HID), norm_ref[0, 0], F32)
    scale = jnp.minimum(1.0, CLIP_AT / (norm + 1e-06))
    small = small_ref[...]
    rows_own = b_ref.shape[1]
    peep_own = p_ref.shape[1]
    flat = (at_b * nrow + at_r) * rows_own
    lane_back = lax.rem(HID - flat % HID, HID)
    tile_row = lax.broadcasted_iota(jnp.int32, (8, HID), 0)
    picked = jnp.where(tile_row == 4 + flat // HID, small, 0.0)
    picked = jnp.sum(pltpu.roll(picked, lane_back, 1), axis=0, keepdims=True)
    new = adamw_update(b_ref[...], picked[:, 0:rows_own], b1_ref[...], b2_ref[...], scale[:, 0:rows_own])
    bo[...], b1o[...], b2o[...] = new
    shifted = pltpu.roll(small, lax.rem(HID - at_b * peep_own, HID), 1)
    new = adamw_update(p_ref[...], shifted[0:3, 0:peep_own], p1_ref[...], p2_ref[...], scale[:, 0:peep_own])
    po[...], p1o[...], p2o[...] = new
    new = adamw_update(k_ref[...], sum_ref[...], k1_ref[...], k2_ref[...], scale[:, 0:1])
    ko[...], k1o[...], k2o[...] = new
    for i in range(len(fetch)):
        fetch[i].wait()
        put[i].start()
    for c in put:
        c.wait()


def local(
    nbat,
    nrow,
    frames,
    crop_sizes,
    kernel,
    gate_bias,
    peepholes,
    cotangent,
    kernel_first,
    kernel_second,
    bias_first,
    bias_second,
    peep_first,
    peep_second,
):
    frames_n, rows_n = frames.shape[1], frames.shape[3]
    pix = rows_n * WID
    own = kernel.shape[1]
    nlow = max(1, UNIT // own)
    ncore = 2 if nrow > nlow else 1
    nmid = 2 * (nrow // (nlow * ncore))
    nfar = nbat // 2
    at_r = lax.axis_index("rows")

    kt = kernel.T
    if nlow > 1:
        kt = lax.dynamic_update_slice(
            jnp.zeros((UNIT, KROWS), F32), kt, (lax.rem(at_r, nlow) * own, 0)
        )
    bias_row = gate_bias.reshape(1, own)

    vm = pltpu.VMEM
    part = (UNIT, PART)
    pair = (nfar, nmid) if ncore > 1 else (1, 1)
    acc_shapes = [
        [vm((nfar, nmid, ncore) + part, F32), vm(pair + part, F32)] for _ in range(3)
    ]
    ncopies = (
        3 * (nfar + nmid + ncore + nlow - 4)
        + 4 * (nfar + nmid + ncore - 3)
        + 3 * (nfar + nmid + ncore - 3)
        + 4
        + 4 * (frames_n - 1)
        + 2 * (nlow - 1)
    )
    scratch = [
        vm((nfar, nmid, ncore, UNIT, KALL), BF16),
        vm((FPAD, GATES), BF16),
        vm((frames_n, rows_n + 2, CIN, WID), F32),
        vm((frames_n, WIDE + FEAT, (rows_n + 2) * WID), BF16),
        vm((frames_n - 1, rows_n + 2, WID, WIDE), BF16),
        vm((frames_n, pix, GATES), F32),
        vm((frames_n, pix, HID), F32),
        vm((frames_n, pix, GATES), BF16),
        vm((rows_n + 2, WID, HID), F32),
        vm((frames_n, rows_n, WID, HID), BF16),
        vm((WID, HID), F32),
        vm((8, HID), F32),
        vm((7, 8, HID), F32),
        acc_shapes,
        vm((9 * CIN, GATES), F32),
        vm((frames_n, CIN, rows_n, WID), F32),
        vm((2, frames_n, CIN, WID), BF16),
        vm((2, frames_n, CIN, WID), BF16),
        vm((frames_n - 1, 2, WID, HID), BF16),
        vm((frames_n - 1, 2, WID, HID), BF16),
        vm((frames_n - 1, 2, WID, HID), BF16),
        vm((2, frames_n, CIN, WID), BF16),
        vm((2, frames_n, CIN, WID), BF16),
        vm((UNIT, KALL), F32),
    ]
    scratch += [vm(pair + part, BF16)] * 6
    scratch += [vm((nmid - 1, nfar) + part, BF16)] * 6
    scratch += [vm((nfar,) + part, BF16)] * 3 + [vm((nfar - 1,) + part, BF16)] * 3
    scratch += [vm((3, size, 8, HID), F32) for size in (nfar, nmid, ncore, nlow)]
    scratch += [vm((UNIT, KALL), BF16), vm((2, max(1, nlow - 1), UNIT, KALL), BF16)]
    scratch += [
        pltpu.SemaphoreType.DMA((ncopies,)),
        pltpu.SemaphoreType.DMA((ncopies,)),
        pltpu.SemaphoreType.DMA((2 + frames_n,)),
    ]
    smem = pl.BlockSpec(memory_space=pltpu.SMEM)
    vmem = pl.BlockSpec(memory_space=pltpu.VMEM)
    hbm = pl.BlockSpec(memory_space=pl.ANY)
    dims = (nbat, nrow, frames_n, rows_n, nfar, nmid, ncore, nlow)
    hidden, frames_back, kernel_sum, small_sum, norm = pl.pallas_call(
        functools.partial(layer_kernel, dims),
        out_shape=(
            jax.ShapeDtypeStruct(cotangent.shape, BF16),
            jax.ShapeDtypeStruct(frames.shape, F32),
            jax.ShapeDtypeStruct((UNIT, KROWS), F32),
            jax.ShapeDtypeStruct((8, HID), F32),
            jax.ShapeDtypeStruct((8, HID), F32),
        ),
        in_specs=[smem, vmem, vmem, vmem, vmem, hbm],
        out_specs=(hbm, hbm, vmem, vmem, vmem),
        scratch_shapes=scratch,
        compiler_params=pltpu.CompilerParams(
            collective_id=0, has_side_effects=True, vmem_limit_bytes=63 << 20
        ),
        name="layer",
    )(crop_sizes, frames, kt, bias_row, peepholes, cotangent)

    if nlow > 1:
        kernel_sum = lax.dynamic_slice_in_dim(kernel_sum, lax.rem(at_r, nlow) * own, own, 0)
    kshape = jax.ShapeDtypeStruct((own, KROWS), F32)
    bshape = jax.ShapeDtypeStruct((1, own), F32)
    pshape = jax.ShapeDtypeStruct(peepholes.shape, F32)
    outs = pl.pallas_call(
        functools.partial(update_kernel, (nbat, nrow)),
        out_shape=(
            jax.ShapeDtypeStruct(cotangent.shape, BF16),
            jax.ShapeDtypeStruct(frames.shape, F32),
            jax.ShapeDtypeStruct((1, 1), F32),
        )
        + (kshape,) * 3 + (bshape,) * 3 + (pshape,) * 3,
        in_specs=[hbm, hbm, smem] + [vmem] * 11,
        out_specs=(hbm, hbm, smem) + (vmem,) * 9,
        scratch_shapes=[
            pltpu.VMEM(cotangent.shape[1:], BF16),
            pltpu.VMEM(frames.shape[1:], F32),
            pltpu.SemaphoreType.DMA((4, frames_n)),
        ],
        compiler_params=pltpu.CompilerParams(vmem_limit_bytes=63 << 20),
        name="update",
    )(
        hidden, frames_back, norm, kernel_sum, small_sum,
        kernel.T, bias_row, peepholes, kernel_first.T, kernel_second.T,
        bias_first.reshape(1, own), bias_second.reshape(1, own), peep_first, peep_second,
    )
    hidden_seq, frames_grad, norm = outs[:3]
    kernels, biases, peeps = outs[3:6], outs[6:9], outs[9:]
    return (
        hidden_seq,
        frames_grad,
        norm[0, 0],
        *(k.T for k in kernels),
        *(v.reshape(own) for v in biases),
        *peeps,
    )


def solution(mesh):
    return jax.shard_map(
        functools.partial(local, mesh.shape["batch"], mesh.shape["rows"]),
        mesh=mesh,
        in_specs=(
            P("batch", None, None, "rows", None),
            P("batch", None),
            P(None, ("batch", "rows")),
            P(("batch", "rows")),
            P(None, "batch"),
            P("batch", None, "rows", None, None),
            P(None, ("batch", "rows")),
            P(None, ("batch", "rows")),
            P(("batch", "rows")),
            P(("batch", "rows")),
            P(None, "batch"),
            P(None, "batch"),
        ),
        out_specs=(
            P("batch", None, "rows", None, None),
            P("batch", None, None, "rows", None),
            P(),
            P(None, ("batch", "rows")),
            P(None, ("batch", "rows")),
            P(None, ("batch", "rows")),
            P(("batch", "rows")),
            P(("batch", "rows")),
            P(("batch", "rows")),
            P(None, "batch"),
            P(None, "batch"),
            P(None, "batch"),
        ),
        check_vma=False,
    )
```

```python
import functools

import jax
import jax.numpy as jnp
from jax import lax
from jax.experimental import pallas as pl
from jax.experimental.pallas import tpu as pltpu
from jax.sharding import PartitionSpec as P

CIN = 16
HID = 128
GATES = 512
KROWS = 1296
WID = 128
STEP = 5
CLIP_AT = 0.02
LEARN_RATE = 0.02
BETA_ONE = 0.9
BETA_TWO = 0.999
WEIGHT_DECAY = 0.01
ADAM_EPS = 1e-08

F32 = jnp.float32
BF16 = jnp.bfloat16
MESH = pl.DeviceIdType.MESH
NT = (((1,), (1,)), ((), ()))
NN = (((1,), (0,)), ((), ()))

WIDE = 3 * HID
HALL = 3 * WIDE
FEAT = 3 * CIN
FPAD = 256
KALL = HALL + FPAD
PART = 512
SUB = 32
UNIT = 16


def sigmoid(v):
    return 0.5 * jnp.tanh(0.5 * v) + 0.5


def mm(a, b, dims):
    return lax.dot_general(a, b, dims, preferred_element_type=F32)


def layer_kernel(
    dims,
    crop_ref,
    frames_ref,
    kt_ref,
    bias_ref,
    peep_ref,
    cot_hbm,
    hid_hbm,
    fg_hbm,
    grad_ref,
    small_out,
    norm_out,
    wt,
    wft,
    fr,
    xt,
    xt0,
    sc,
    gates,
    cells,
    gpre,
    gs,
    cot,
    consts,
    sums,
    acc,
    fzero,
    fgo,
    fhalo_s,
    fhalo_r,
    shalo_r,
    ghalo_s,
    ghalo_r,
    bhalo_s,
    bhalo_r,
    nat,
    *rest,
):
    nbat, nrow, frames_n, rows_n, nfar, nmid, ncore, nlow = dims
    pix = rows_n * WID
    rest = list(rest)
    core_send, core_recv, mid_send, mid_recv, far_send, far_recv = (
        [rest.pop(0) for _ in range(3)] for _ in range(6)
    )
    small_bufs = [rest.pop(0) for _ in range(4)]
    low_send, low_recv = rest.pop(0), rest.pop(0)
    norm_tiles, nsems = rest.pop(0), rest.pop(0)
    sems = rest.pop(0)
    rsems = rest.pop(0)
    lsems = rest.pop(0)

    at_b = lax.axis_index("batch")
    at_r = lax.axis_index("rows")
    counter = [0]
    pending = []

    def remote(src, dst, bat, row):
        i = counter[0]
        counter[0] += 1
        c = pltpu.make_async_remote_copy(
            src_ref=src, dst_ref=dst, send_sem=sems.at[i], recv_sem=rsems.at[i],
            device_id=(bat, row), device_id_type=MESH,
        )
        c.start()
        pending.append(c)
        return c

    far, near = at_b // 2, at_b % 2
    low = at_r % nlow
    core = (at_r // nlow) % ncore
    half = nmid // 2
    mid = near * half + at_r // (nlow * ncore)

    def device(f, m, c, w):
        return (f * 2 + m // half, ((m % half) * ncore + c) * nlow + w)

    def far_peer(k):
        return device(lax.rem(far + k, nfar), mid, core, low)

    def mid_peer(k):
        return device(far, lax.rem(mid + k, nmid), core, low)

    def core_peer(k):
        return device(far, mid, lax.rem(core + k, ncore), low)

    def low_peer(k):
        return device(far, mid, core, lax.rem(low + k, nlow))

    groups = [(nfar, far_peer, far), (nmid, mid_peer, mid), (ncore, core_peer, core), (nlow, low_peer, low)]
    up_r = lax.rem(at_r + nrow - 1, nrow)
    down_r = lax.rem(at_r + 1, nrow)

    barrier = pltpu.get_barrier_semaphore()
    ndev = nbat * nrow
    me = at_b * nrow + at_r

    def any_peer(k):
        to = lax.rem(me + k, ndev)
        return (to // nrow, lax.rem(to, nrow))

    def greet(k, carry):
        pl.semaphore_signal(barrier, inc=1, device_id=any_peer(k), device_id_type=MESH)
        return carry

    lax.fori_loop(1, ndev, greet, 0)

    cot_copy = pltpu.make_async_copy(cot_hbm.at[0], cot, lsems.at[0])
    cot_copy.start()

    ktv = kt_ref[...]
    own = []
    for tap in range(9):
        own.append(ktv[:, tap * (CIN + HID) + CIN : (tap + 1) * (CIN + HID)])
    for tap in range(9):
        own.append(ktv[:, tap * (CIN + HID) : tap * (CIN + HID) + CIN])
    own.append(jnp.zeros((UNIT, FPAD - 9 * CIN), F32))
    wt[far, mid, core] = jnp.concatenate(own, axis=1).astype(BF16)

    rows_own = GATES // (nbat * nrow)
    flat = (at_b * nrow + at_r) * rows_own
    peep_own = HID // nbat
    tile_row = lax.broadcasted_iota(jnp.int32, (8, HID), 0)
    consts[...] = jnp.zeros_like(consts)
    consts[0:3, 0:peep_own] = peep_ref[...]
    consts[4:5, 0:rows_own] = bias_ref[...]
    peep_tile = pltpu.roll(jnp.where(tile_row < 3, consts[...], 0.0), at_b * peep_own, 1)
    bias_tile = pltpu.roll(jnp.broadcast_to(consts[4:5, :], (8, HID)), flat % HID, 1)
    bias_tile = jnp.where(tile_row == 4 + flat // HID, bias_tile, 0.0)
    start_tile = jnp.where(at_r == 0, peep_tile, 0.0) + bias_tile

    small_step = [0] * 2
    small_moving = [None] * 2

    def small_next(i, tile=None):
        s = small_step[i]
        small_step[i] = s + 1
        while s < 4 and groups[s][0] == 1:
            s += 1
            small_step[i] = s + 1
        if tile is None:
            done = s - 1
            while groups[done][0] == 1:
                done -= 1
            for c in small_moving[i]:
                c.wait_recv()
            tile = small_bufs[done][i, 0]
            for k in range(1, groups[done][0]):
                tile = tile + small_bufs[done][i, k]
        if s < 4:
            size, peer, place = groups[s]
            ref = small_bufs[s].at[i, place]
            ref[...] = tile
            small_moving[i] = [remote(ref, ref, *peer(k)) for k in range(1, size)]
            return None
        return tile

    def small_finish(i):
        while True:
            tile = small_next(i)
            if tile is not None:
                return tile

    lanes = [(HALL, KALL), (0, WIDE), (WIDE, 2 * WIDE), (2 * WIDE, HALL)]
    steps = [0] * 4
    moving = [None] * 4

    def gather_low():
        if nlow > 1:
            low_send[...] = wt[far, mid, core]
            copies = [remote(low_send, low_recv.at[0, k - 1], *low_peer(k)) for k in range(1, nlow)]
            total = low_send[...]
            for k in range(1, nlow):
                copies[k - 1].wait_recv()
                total = total + low_recv[0, k - 1]
            wt[far, mid, core] = total

    def gather_step(i):
        lo, up = lanes[i]
        cols = pl.ds(lo, up - lo)
        s = steps[i]
        steps[i] = s + 1
        if 0 < s < 4:
            for c in moving[i]:
                c.wait_recv()
        if s < 3:
            size, peer, _ = groups[s]
            if s == 0:
                ref = wt.at[far, mid, core, :, cols]
            elif s == 1:
                ref = wt.at[:, mid, core, :, cols]
            else:
                ref = wt.at[:, :, core, :, cols]
            moving[i] = [remote(ref, ref, *peer(k)) for k in range(1, size)]

    crop_h = crop_ref[0, 0]
    crop_w = crop_ref[0, 1]
    row0 = at_r * rows_n
    has_up = (at_r > 0).astype(F32)
    has_down = (at_r < nrow - 1).astype(F32)

    rr3 = lax.broadcasted_iota(jnp.int32, (CIN, rows_n, WID), 1) + row0
    cc3 = lax.broadcasted_iota(jnp.int32, (CIN, rows_n, WID), 2)
    live3 = (rr3 < crop_h) & (cc3 < crop_w)
    for t in range(frames_n):
        masked = jnp.where(live3, frames_ref[0, t].astype(F32), 0.0)
        fr[t, 1 : rows_n + 1] = jnp.swapaxes(masked, 0, 1)
        fhalo_s[0, t] = fr[t, 1].astype(BF16)
        fhalo_s[1, t] = fr[t, rows_n].astype(BF16)

    def lane_shift(v, by):
        at = lax.broadcasted_iota(jnp.int32, v.shape, 1)
        if by > 0:
            return jnp.where(at == WID - 1, 0.0, pltpu.roll(v, WID - 1, 1))
        return jnp.where(at == 0, 0.0, pltpu.roll(v, 1, 1))

    def row_shift(v, by):
        at = lax.broadcasted_iota(jnp.int32, v.shape, 0)
        if by > 0:
            return jnp.where(at == WID - 1, 0.0, pltpu.roll(v, WID - 1, 0))
        return jnp.where(at == 0, 0.0, pltpu.roll(v, 1, 0))

    def frame_part(t):
        return xt.at[t - 1, WIDE : WIDE + FEAT] if t > 0 else xt0

    def frame_cols(t, rr):
        v = fr[t, rr]
        three = jnp.concatenate([lane_shift(v, -1), v, lane_shift(v, 1)], axis=0)
        frame_part(t)[:, pl.ds(pl.multiple_of(rr * WID, WID), WID)] = three.astype(BF16)

    def frame_cols_all(rr, carry):
        for t in range(frames_n):
            frame_cols(t, rr)
        return carry

    def frame_pixels(t, lo, up):
        def one(rr, carry):
            parts = [
                frame_part(t)[:, pl.ds(pl.multiple_of((rr + a) * WID, WID), WID)].astype(F32)
                for a in range(3)
            ]
            parts.append(jnp.zeros((FPAD - 9 * CIN, WID), F32))
            gpre[t, pl.ds(pl.multiple_of(rr * WID, WID), WID), 0:FPAD] = (
                jnp.concatenate(parts, axis=0).T.astype(BF16)
            )
            return carry

        lax.fori_loop(lo, up, one, 0)

    lax.fori_loop(1, rows_n + 1, frame_cols_all, 0)
    frame_pixels(0, 1, rows_n - 1)

    pl.semaphore_wait(barrier, ndev - 1)
    gather_low()
    gather_step(0)
    small_next(0, start_tile)
    f_up = remote(fhalo_s.at[0], fhalo_r.at[1], at_b, up_r)
    f_down = remote(fhalo_s.at[1], fhalo_r.at[0], at_b, down_r)
    gather_step(1)
    gather_step(2)
    gather_step(3)
    if frames_n > 1:
        frame_pixels(1, 1, rows_n - 1)
    gather_step(0)
    small_next(0)
    f_up.wait_recv()
    f_down.wait_recv()
    for t in range(frames_n):
        fr[t, 0] = fhalo_r[0, t].astype(F32) * has_up
        fr[t, rows_n + 1] = fhalo_r[1, t].astype(F32) * has_down
        frame_cols(t, 0)
        frame_cols(t, rows_n + 1)
    for t in range(min(2, frames_n)):
        frame_pixels(t, 0, 1)
        frame_pixels(t, rows_n - 1, rows_n)
    gather_step(1)
    if frames_n > 2:
        frame_pixels(2, 0, rows_n)
    gather_step(2)
    gather_step(0)
    small_next(0)
    gather_step(3)
    for t in range(3, frames_n):
        frame_pixels(t, 0, rows_n)
    gather_step(0)

    consts[...] = small_finish(0)
    peep = [consts[i : i + 1, :] for i in range(3)]
    bias = [consts[4 + i : 5 + i, :] for i in range(4)]

    def cat_wt(lo, up):
        return wt[:, :, :, :, lo:up].reshape(GATES, up - lo)

    sub_iota = lax.broadcasted_iota(jnp.int32, (SUB, HID), 0)

    def live_cols(rr):
        return jnp.where(row0 + rr < crop_h, crop_w, 0)

    def place_state(t, v, at):
        three = [row_shift(v, -1), v, row_shift(v, 1)]
        for j in range(3):
            low_j = three[j].astype(BF16)
            sc[t, at, :, j * HID : (j + 1) * HID] = low_j
            xt[t, j * HID : (j + 1) * HID, at * WID : (at + 1) * WID] = low_j.T

    CH = 4
    nchunk = rows_n // CH

    def forward_dot(t, m):
        px = pl.ds(m * CH * WID, CH * WID)
        xf = gpre[t, px, 0:FPAD]
        if t > 0:
            parts = [sc[t - 1, m * CH + a : m * CH + a + CH].reshape(CH * WID, WIDE) for a in range(3)]
            x = jnp.concatenate(parts + [xf], axis=1)
            gates[t, px, :] = mm(x, cat_wt(0, KALL), NT)
        else:
            gates[t, px, :] = mm(xf, cat_wt(HALL, KALL), NT)

    def forward_rows(t, m):
        for rr in range(m * CH, (m + 1) * CH):
            limit = live_cols(rr)
            state = []
            for j in range(WID // SUB):
                sl = pl.ds(rr * WID + j * SUB, SUB)
                live = sub_iota + j * SUB < limit
                zi = gates[t, sl, 0:HID] + bias[0]
                zc = gates[t, sl, 2 * HID : 3 * HID] + bias[2]
                zo = gates[t, sl, 3 * HID :] + bias[3]
                if t > 0:
                    prev = cells[t - 1, sl, :]
                    zf = gates[t, sl, HID : 2 * HID] + bias[1] + peep[1] * prev
                    zi = zi + peep[0] * prev
                    gf = sigmoid(zf)
                    gates[t, sl, HID : 2 * HID] = gf
                gi = sigmoid(zi)
                gc = jnp.tanh(zc)
                c = gi * gc
                if t > 0:
                    c = c + gf * prev
                c = jnp.where(live, c, 0.0)
                go = sigmoid(zo + peep[2] * c)
                gates[t, sl, 0:HID] = gi
                gates[t, sl, 2 * HID : 3 * HID] = gc
                gates[t, sl, 3 * HID :] = go
                cells[t, sl, :] = c
                state.append(jnp.where(live, go * jnp.tanh(c), 0.0))
            state = jnp.concatenate(state, axis=0)
            if t < frames_n - 1:
                place_state(t, state, rr + 1)
            else:
                sc[0, rr + 1, :, 0:HID] = state.astype(BF16)

    hid_copies = []
    center = pl.ds(HID, HID)
    halos = [[None, None] for _ in range(frames_n)]

    def state_done(t, m):
        if t < frames_n - 1 and m == 0:
            halos[t][1] = remote(sc.at[t, 1, :, center], shalo_r.at[t, 1], at_b, up_r)
        if t < frames_n - 1 and m == nchunk - 1:
            halos[t][0] = remote(sc.at[t, rows_n, :, center], shalo_r.at[t, 0], at_b, down_r)
        if (t, m) == last_of[t]:
            lanes_of = center if t < frames_n - 1 else pl.ds(0, HID)
            src = sc.at[t if t < frames_n - 1 else 0, pl.ds(1, rows_n), :, lanes_of]
            c = pltpu.make_async_copy(src, hid_hbm.at[0, t], lsems.at[1 + t])
            c.start()
            hid_copies.append(c)

    order = list(range(1, nchunk - 1)) + [0, nchunk - 1]
    slots = [(0, m) for m in range(nchunk)] + [(t, m) for t in range(1, frames_n) for m in order]
    last_of = {t: [s for s in slots if s[0] == t][-1] for t in range(frames_n)}
    for i, (t, m) in enumerate(slots + [(frames_n, 0)]):
        if t == 1 and m == order[0]:
            for k in range(1, 4):
                while steps[k] < 4:
                    gather_step(k)
        if 0 < t < frames_n and m == order[nchunk - 2]:
            for k in range(2):
                halos[t - 1][k].wait_recv()
            place_state(t - 1, shalo_r[t - 1, 0].astype(F32) * has_up, 0)
            place_state(t - 1, shalo_r[t - 1, 1].astype(F32) * has_down, rows_n + 1)
        if t < frames_n:
            forward_dot(t, m)
        if i > 0:
            forward_rows(*slots[i - 1])
            state_done(*slots[i - 1])
        if t == 0 and 0 < m < 4:
            gather_step(m)

    cot_copy.wait()
    sums[...] = jnp.zeros_like(sums)

    def fold(v):
        return jnp.sum(v.reshape(SUB // 8, 8, HID), axis=0)

    def backward_rows(t, m):
        parts = [None] * 7
        for rr in range(m * CH, (m + 1) * CH):
            limit = live_cols(rr)
            for j in range(WID // SUB):
                cols = slice(j * SUB, (j + 1) * SUB)
                sl = pl.ds(rr * WID + j * SUB, SUB)
                live = sub_iota + j * SUB < limit
                gi = gates[t, sl, 0:HID]
                gc = gates[t, sl, 2 * HID : 3 * HID]
                go = gates[t, sl, 3 * HID :]
                c = cells[t, sl, :]
                sq = jnp.tanh(c)
                total = cot[t, rr, cols, :].astype(F32)
                if t < frames_n - 1:
                    total = total + gs[(t + 1) % 2, rr + 1, cols, :]
                    if rr == 0:
                        total = total + ghalo_r[t, 0, cols, :].astype(F32) * has_up
                    if rr == rows_n - 1:
                        total = total + ghalo_r[t, 1, cols, :].astype(F32) * has_down
                total = jnp.where(live, total, 0.0)
                tgo = total * go
                d_out = tgo * sq * (1.0 - go)
                nxt = tgo * (1.0 - sq * sq) + peep[2] * d_out
                if t < frames_n - 1:
                    nxt = nxt + cells[t + 1, sl, :]
                kept = jnp.where(live, nxt, 0.0)
                kgi = kept * gi
                d_in = kgi * gc * (1.0 - gi)
                d_cand = kgi * (1.0 - gc * gc)
                vals = [d_in, None, d_cand, d_out, None, None, d_out * c]
                if t > 0:
                    gf = gates[t, sl, HID : 2 * HID]
                    prev = cells[t - 1, sl, :]
                    kgf = kept * gf
                    d_for = kgf * prev * (1.0 - gf)
                    cells[t, sl, :] = kgf + peep[0] * d_in + peep[1] * d_for
                    vals[1] = d_for
                    vals[4] = d_in * prev
                    vals[5] = d_for * prev
                gpre[t, sl, 0:HID] = d_in.astype(BF16)
                gpre[t, sl, HID : 2 * HID] = (vals[1] if t > 0 else jnp.zeros_like(d_in)).astype(BF16)
                gpre[t, sl, 2 * HID : 3 * HID] = d_cand.astype(BF16)
                gpre[t, sl, 3 * HID :] = d_out.astype(BF16)
                for i in range(7):
                    if vals[i] is not None:
                        f = fold(vals[i])
                        parts[i] = f if parts[i] is None else parts[i] + f
        for i in range(7):
            if parts[i] is not None:
                sums[i] = sums[i] + parts[i]

    def state_chunk(t, m, done):
        y = mm(gpre[t, m * CH * WID : (m + 1) * CH * WID, :], cat_wt(0, HALL), NN)
        row = [None] * (CH + 2)
        for i in range(CH):
            for a in range(3):
                three = [y[i * WID : (i + 1) * WID, a * WIDE + j * HID : a * WIDE + (j + 1) * HID] for j in range(3)]
                z = three[1] + row_shift(three[0], 1) + row_shift(three[2], -1)
                row[i + a] = z if row[i + a] is None else row[i + a] + z
        for k in range(CH + 2):
            at = m * CH + k
            gs[t % 2, at] = gs[t % 2, at] + row[k] if at in done else row[k]
            done.add(at)

    work = [(t, m) for t in reversed(range(frames_n)) for m in order]
    backward_rows(*work[0])
    ghalos = [[None, None] for _ in range(frames_n)]

    def rows_ready(t, m):
        if t < frames_n - 1 and m in (0, nchunk - 1):
            ghalos[t + 1][0 if m == 0 else 1].wait_recv()

    written = {t: set() for t in range(frames_n)}
    for i, (t, m) in enumerate(work):
        if t == 0:
            break
        rows_ready(*work[i + 1])
        state_chunk(t, m, written[t])
        backward_rows(*work[i + 1])
        if m == 0:
            ghalo_s[t - 1, 0] = gs[t % 2, 0].astype(BF16)
            ghalos[t][1] = remote(ghalo_s.at[t - 1, 0], ghalo_r.at[t - 1, 1], at_b, up_r)
        if m == nchunk - 1:
            ghalo_s[t - 1, 1] = gs[t % 2, rows_n + 1].astype(BF16)
            ghalos[t][0] = remote(ghalo_s.at[t - 1, 1], ghalo_r.at[t - 1, 0], at_b, down_r)
    left = work[-(nchunk - 1) :]

    stage = [0] * 3
    flight = [None] * 3
    parts = [[acc[q][0], acc[q][1] if ncore > 1 else acc[q][0].at[:, :, 0]] for q in range(3)]

    def reduce_step(q):
        s = stage[q]
        stage[q] = s + 1
        first, second = parts[q]
        if s == 0 and ncore > 1:
            core_send[q][...] = first[:, :, 1 - core].astype(BF16)
            flight[q] = [remote(core_send[q], core_recv[q], *core_peer(1))]
        elif s == 1:
            if ncore > 1:
                flight[q][0].wait_recv()
                second[...] = first[:, :, core] + core_recv[q][...].astype(F32)
            flight[q] = []
            for k in range(1, nmid):
                to = lax.rem(mid + k, nmid)
                mid_send[q][k - 1] = second[:, to].astype(BF16)
                flight[q].append(remote(mid_send[q].at[k - 1], mid_recv[q].at[k - 1], *mid_peer(k)))
        elif s == 2:
            total = second[:, mid]
            for k in range(1, nmid):
                flight[q][k - 1].wait_recv()
                total = total + mid_recv[q][k - 1].astype(F32)
            second[:, mid] = total
            far_send[q][...] = total.astype(BF16)
            flight[q] = []
            for k in range(1, nfar):
                to = lax.rem(far + k, nfar)
                flight[q].append(remote(far_send[q].at[to], far_recv[q].at[k - 1], *far_peer(k)))
        elif s == 3:
            total = second[far, mid]
            for k in range(1, nfar):
                flight[q][k - 1].wait_recv()
                total = total + far_recv[q][k - 1].astype(F32)
            for j in range(3):
                at = (3 * q + j) * (CIN + HID)
                nat[:, at : at + CIN] = total[:, WIDE + j * CIN : WIDE + (j + 1) * CIN]
                nat[:, at + CIN : at + CIN + HID] = total[:, j * HID : (j + 1) * HID]

    def kernel_dot(a, t):
        return mm(xt[t - 1, :, a * WID : a * WID + pix], gpre[t], NN)

    def finish_rows(k):
        rows_ready(*left[k])
        backward_rows(*left[k])

    def place_chunk(a, total):
        extra = total[WIDE:, :] + fzero[a * FEAT : (a + 1) * FEAT, :]
        whole = jnp.concatenate([total[:WIDE, :], extra, jnp.zeros((PART - WIDE - FEAT, GATES), F32)], axis=0)
        acc[a][0][...] = whole.T.reshape(acc[a][0].shape)

    totals = [None] * 3
    for a in range(3):
        for t in range(1, frames_n):
            part = kernel_dot(a, t)
            totals[a] = part if t == 1 else totals[a] + part
            if a == 0 and t - 1 < len(left):
                finish_rows(t - 1)
            if a > 0 and t == 1:
                place_chunk(a - 1, totals[a - 1])
                reduce_step(a - 1)
            if a > 0 and t == 2:
                if a > 1:
                    reduce_step(a - 2)
                reduce_step(a - 1)
                small_next(1)
        if a == 0:
            for k in range(frames_n - 1, len(left)):
                finish_rows(k)
            g0 = [xt0[:, k * WID : k * WID + pix] for k in range(3)]
            fzero[...] = mm(jnp.concatenate(g0, axis=0), gpre[0], NN)
            rows = [jnp.sum(sums[i], axis=0, keepdims=True) for i in range(7)]
            small_next(1, jnp.concatenate(rows[4:] + [jnp.zeros((1, HID), F32)] + rows[:4], axis=0))
    place_chunk(2, totals[2])
    reduce_step(2)

    fgb = fr

    def frame_back(t):
        fgb[t] = jnp.zeros(fgb.shape[1:], F32)

        def chunk(m, carry):
            px = pl.ds(pl.multiple_of(m * CH * WID, CH * WID), CH * WID)
            y = mm(wft[0 : 9 * CIN, :], gpre[t, px, :], NT)
            for i in range(CH):
                for a in range(3):
                    part = y[a * FEAT : (a + 1) * FEAT, i * WID : (i + 1) * WID]
                    z = part[CIN : 2 * CIN]
                    z = z + lane_shift(part[0:CIN], 1)
                    z = z + lane_shift(part[2 * CIN :], -1)
                    at = m * CH + i + a
                    fgb[t, at] = fgb[t, at] + z
            return carry

        lax.fori_loop(0, nchunk, chunk, 0)
        bhalo_s[0, t] = fgb[t, 0].astype(BF16)
        bhalo_s[1, t] = fgb[t, rows_n + 1].astype(BF16)

    wft[...] = cat_wt(HALL, KALL).astype(F32).T.astype(BF16)
    after = [[2], [1, 0], [], []]
    for t in range(frames_n):
        frame_back(t)
        for q in after[t] if t < 4 else []:
            reduce_step(q)
    f_up = remote(bhalo_s.at[0], bhalo_r.at[1], at_b, up_r)
    f_down = remote(bhalo_s.at[1], bhalo_r.at[0], at_b, down_r)
    for q in (2, 1, 0):
        while stage[q] < 3:
            reduce_step(q)
    for q in range(3):
        while stage[q] < 4:
            reduce_step(q)
    if nlow > 1:
        low_send[...] = nat[...].astype(BF16)
        copies = [remote(low_send, low_recv.at[1, k - 1], *low_peer(k)) for k in range(1, nlow)]
        total = nat[...]
        for k in range(1, nlow):
            copies[k - 1].wait_recv()
            total = total + low_recv[1, k - 1].astype(F32)
        nat[...] = total

    g = nat[:, 0:KROWS]
    squares = g * g
    if nlow > 1:
        base = low * rows_own
        ri = lax.broadcasted_iota(jnp.int32, squares.shape, 0)
        squares = jnp.where((ri >= base) & (ri < base + rows_own), squares, 0.0)
    norm_tiles[me] = jnp.broadcast_to(jnp.sum(squares), (8, HID))

    def norm_copy(k):
        row = norm_tiles.at[me, 0:1]
        return pltpu.make_async_remote_copy(
            src_ref=row, dst_ref=row, send_sem=nsems.at[0, k], recv_sem=nsems.at[1, k],
            device_id=any_peer(k), device_id_type=MESH,
        )

    lax.fori_loop(1, ndev, lambda k, c: (norm_copy(k).start(), c)[1], 0)
    grad_ref[...] = g
    small = small_finish(1)
    small_out[...] = small
    f_up.wait_recv()
    f_down.wait_recv()
    for t in range(frames_n):
        fgb[t, 1] = fgb[t, 1] + bhalo_r[0, t].astype(F32) * has_up
        fgb[t, rows_n] = fgb[t, rows_n] + bhalo_r[1, t].astype(F32) * has_down
        fgo[t] = jnp.where(live3, jnp.swapaxes(fgb[t, 1 : rows_n + 1], 0, 1), 0.0)
    c = pltpu.make_async_copy(fgo, fg_hbm.at[0], lsems.at[1 + frames_n])
    c.start()
    hid_copies.append(c)
    lax.fori_loop(1, ndev, lambda k, c: (norm_copy(k).wait_recv(), c)[1], 0)
    squares = jnp.sum(norm_tiles[:, 0:1, :], axis=0) + jnp.sum(small * small)
    norm_out[...] = jnp.broadcast_to(jnp.sqrt(squares), (8, HID))
    lax.fori_loop(1, ndev, lambda k, c: (norm_copy(k).wait_send(), c)[1], 0)

    for c in hid_copies:
        c.wait()
    for c in pending:
        c.wait_send()


def adamw_update(weight, gradient, first, second, scale):
    clipped = gradient * scale
    first_new = BETA_ONE * first + (1.0 - BETA_ONE) * clipped
    second_new = BETA_TWO * second + (1.0 - BETA_TWO) * clipped * clipped
    first_hat = first_new / (1.0 - BETA_ONE**STEP)
    second_hat = second_new / (1.0 - BETA_TWO**STEP)
    weight_new = weight - LEARN_RATE * (
        first_hat / (jnp.sqrt(second_hat) + ADAM_EPS) + WEIGHT_DECAY * weight
    )
    return (weight_new, first_new, second_new)


def update_kernel(
    dims, hid_in, fg_in, norm_ref, sum_ref, small_ref,
    k_ref, b_ref, p_ref, k1_ref, k2_ref, b1_ref, b2_ref, p1_ref, p2_ref,
    hid_out, fg_out, norm_out, ko, k1o, k2o, bo, b1o, b2o, po, p1o, p2o, hid_buf, fg_buf, sems,
):
    nbat, nrow = dims
    frames_n = hid_buf.shape[0]
    fetch, put = [], []
    for t in range(frames_n):
        for i, (src, buf, dst) in enumerate(((hid_in, hid_buf, hid_out), (fg_in, fg_buf, fg_out))):
            fetch.append(pltpu.make_async_copy(src.at[0, t], buf.at[t], sems.at[i, t]))
            put.append(pltpu.make_async_copy(buf.at[t], dst.at[0, t], sems.at[2 + i, t]))
    for c in fetch:
        c.start()
    at_b = lax.axis_index("batch")
    at_r = lax.axis_index("rows")
    norm_out[0, 0] = norm_ref[0, 0]
    norm = jnp.full((1, HID), norm_ref[0, 0], F32)
    scale = jnp.minimum(1.0, CLIP_AT / (norm + 1e-06))
    small = small_ref[...]
    rows_own = b_ref.shape[1]
    peep_own = p_ref.shape[1]
    flat = (at_b * nrow + at_r) * rows_own
    lane_back = lax.rem(HID - flat % HID, HID)
    tile_row = lax.broadcasted_iota(jnp.int32, (8, HID), 0)
    picked = jnp.where(tile_row == 4 + flat // HID, small, 0.0)
    picked = jnp.sum(pltpu.roll(picked, lane_back, 1), axis=0, keepdims=True)
    new = adamw_update(b_ref[...], picked[:, 0:rows_own], b1_ref[...], b2_ref[...], scale[:, 0:rows_own])
    bo[...], b1o[...], b2o[...] = new
    shifted = pltpu.roll(small, lax.rem(HID - at_b * peep_own, HID), 1)
    new = adamw_update(p_ref[...], shifted[0:3, 0:peep_own], p1_ref[...], p2_ref[...], scale[:, 0:peep_own])
    po[...], p1o[...], p2o[...] = new
    new = adamw_update(k_ref[...], sum_ref[...], k1_ref[...], k2_ref[...], scale[:, 0:1])
    ko[...], k1o[...], k2o[...] = new
    for i in range(len(fetch)):
        fetch[i].wait()
        put[i].start()
    for c in put:
        c.wait()


def local(
    nbat,
    nrow,
    frames,
    crop_sizes,
    kernel,
    gate_bias,
    peepholes,
    cotangent,
    kernel_first,
    kernel_second,
    bias_first,
    bias_second,
    peep_first,
    peep_second,
):
    frames_n, rows_n = frames.shape[1], frames.shape[3]
    pix = rows_n * WID
    own = kernel.shape[1]
    nlow = max(1, UNIT // own)
    ncore = 2 if nrow > nlow else 1
    nmid = 2 * (nrow // (nlow * ncore))
    nfar = nbat // 2
    at_r = lax.axis_index("rows")

    kt = kernel.T
    if nlow > 1:
        kt = lax.dynamic_update_slice(
            jnp.zeros((UNIT, KROWS), F32), kt, (lax.rem(at_r, nlow) * own, 0)
        )
    bias_row = gate_bias.reshape(1, own)

    vm = pltpu.VMEM
    part = (UNIT, PART)
    pair = (nfar, nmid) if ncore > 1 else (1, 1)
    acc_shapes = [
        [vm((nfar, nmid, ncore) + part, F32), vm(pair + part, F32)] for _ in range(3)
    ]
    ncopies = (
        2 * (nfar + nmid + ncore + nlow - 4)
        + 4 * (nfar + nmid + ncore - 3)
        + 3 * (nfar + nmid + ncore - 3)
        + 4
        + 4 * (frames_n - 1)
        + 2 * (nlow - 1)
    )
    scratch = [
        vm((nfar, nmid, ncore, UNIT, KALL), BF16),
        vm((FPAD, GATES), BF16),
        vm((frames_n, rows_n + 2, CIN, WID), F32),
        vm((frames_n - 1, WIDE + FEAT, (rows_n + 2) * WID), BF16),
        vm((FEAT, (rows_n + 2) * WID), BF16),
        vm((frames_n - 1, rows_n + 2, WID, WIDE), BF16),
        vm((frames_n, pix, GATES), F32),
        vm((frames_n, pix, HID), F32),
        vm((frames_n, pix, GATES), BF16),
        vm((2, rows_n + 2, WID, HID), F32),
        vm((frames_n, rows_n, WID, HID), BF16),
        vm((8, HID), F32),
        vm((7, 8, HID), F32),
        acc_shapes,
        vm((9 * CIN, GATES), F32),
        vm((frames_n, CIN, rows_n, WID), F32),
        vm((2, frames_n, CIN, WID), BF16),
        vm((2, frames_n, CIN, WID), BF16),
        vm((frames_n - 1, 2, WID, HID), BF16),
        vm((frames_n - 1, 2, WID, HID), BF16),
        vm((frames_n - 1, 2, WID, HID), BF16),
        vm((2, frames_n, CIN, WID), BF16),
        vm((2, frames_n, CIN, WID), BF16),
        vm((UNIT, KALL), F32),
    ]
    scratch += [vm(pair + part, BF16)] * 6
    scratch += [vm((nmid - 1, nfar) + part, BF16)] * 6
    scratch += [vm((nfar,) + part, BF16)] * 3 + [vm((nfar - 1,) + part, BF16)] * 3
    scratch += [vm((2, size, 8, HID), F32) for size in (nfar, nmid, ncore, nlow)]
    scratch += [vm((UNIT, KALL), BF16), vm((2, max(1, nlow - 1), UNIT, KALL), BF16)]
    scratch += [vm((nbat * nrow, 8, HID), F32), pltpu.SemaphoreType.DMA((2, nbat * nrow))]
    scratch += [
        pltpu.SemaphoreType.DMA((ncopies,)),
        pltpu.SemaphoreType.DMA((ncopies,)),
        pltpu.SemaphoreType.DMA((2 + frames_n,)),
    ]
    smem = pl.BlockSpec(memory_space=pltpu.SMEM)
    vmem = pl.BlockSpec(memory_space=pltpu.VMEM)
    hbm = pl.BlockSpec(memory_space=pl.ANY)
    dims = (nbat, nrow, frames_n, rows_n, nfar, nmid, ncore, nlow)
    hidden, frames_back, kernel_sum, small_sum, norm = pl.pallas_call(
        functools.partial(layer_kernel, dims),
        out_shape=(
            jax.ShapeDtypeStruct(cotangent.shape, BF16),
            jax.ShapeDtypeStruct(frames.shape, F32),
            jax.ShapeDtypeStruct((UNIT, KROWS), F32),
            jax.ShapeDtypeStruct((8, HID), F32),
            jax.ShapeDtypeStruct((8, HID), F32),
        ),
        in_specs=[smem, vmem, vmem, vmem, vmem, hbm],
        out_specs=(hbm, hbm, vmem, vmem, vmem),
        scratch_shapes=scratch,
        compiler_params=pltpu.CompilerParams(
            collective_id=0, has_side_effects=True, vmem_limit_bytes=63 << 20
        ),
        name="layer",
    )(crop_sizes, frames, kt, bias_row, peepholes, cotangent)

    if nlow > 1:
        kernel_sum = lax.dynamic_slice_in_dim(kernel_sum, lax.rem(at_r, nlow) * own, own, 0)
    kshape = jax.ShapeDtypeStruct((own, KROWS), F32)
    bshape = jax.ShapeDtypeStruct((1, own), F32)
    pshape = jax.ShapeDtypeStruct(peepholes.shape, F32)
    outs = pl.pallas_call(
        functools.partial(update_kernel, (nbat, nrow)),
        out_shape=(
            jax.ShapeDtypeStruct(cotangent.shape, BF16),
            jax.ShapeDtypeStruct(frames.shape, F32),
            jax.ShapeDtypeStruct((1, 1), F32),
        )
        + (kshape,) * 3 + (bshape,) * 3 + (pshape,) * 3,
        in_specs=[hbm, hbm, smem] + [vmem] * 11,
        out_specs=(hbm, hbm, smem) + (vmem,) * 9,
        scratch_shapes=[
            pltpu.VMEM(cotangent.shape[1:], BF16),
            pltpu.VMEM(frames.shape[1:], F32),
            pltpu.SemaphoreType.DMA((4, frames_n)),
        ],
        compiler_params=pltpu.CompilerParams(vmem_limit_bytes=63 << 20),
        name="update",
    )(
        hidden, frames_back, norm, kernel_sum, small_sum,
        kernel.T, bias_row, peepholes, kernel_first.T, kernel_second.T,
        bias_first.reshape(1, own), bias_second.reshape(1, own), peep_first, peep_second,
    )
    hidden_seq, frames_grad, norm = outs[:3]
    kernels, biases, peeps = outs[3:6], outs[6:9], outs[9:]
    return (
        hidden_seq,
        frames_grad,
        norm[0, 0],
        *(k.T for k in kernels),
        *(v.reshape(own) for v in biases),
        *peeps,
    )


def solution(mesh):
    return jax.shard_map(
        functools.partial(local, mesh.shape["batch"], mesh.shape["rows"]),
        mesh=mesh,
        in_specs=(
            P("batch", None, None, "rows", None),
            P("batch", None),
            P(None, ("batch", "rows")),
            P(("batch", "rows")),
            P(None, "batch"),
            P("batch", None, "rows", None, None),
            P(None, ("batch", "rows")),
            P(None, ("batch", "rows")),
            P(("batch", "rows")),
            P(("batch", "rows")),
            P(None, "batch"),
            P(None, "batch"),
        ),
        out_specs=(
            P("batch", None, "rows", None, None),
            P("batch", None, None, "rows", None),
            P(),
            P(None, ("batch", "rows")),
            P(None, ("batch", "rows")),
            P(None, ("batch", "rows")),
            P(("batch", "rows")),
            P(("batch", "rows")),
            P(("batch", "rows")),
            P(None, "batch"),
            P(None, "batch"),
            P(None, "batch"),
        ),
        check_vma=False,
    )
```

```python
import functools

import jax
import jax.numpy as jnp
from jax import lax
from jax.experimental import pallas as pl
from jax.experimental.pallas import tpu as pltpu
from jax.sharding import PartitionSpec as P

CIN = 16
HID = 128
GATES = 512
KROWS = 1296
WID = 128
STEP = 5
CLIP_AT = 0.02
LEARN_RATE = 0.02
BETA_ONE = 0.9
BETA_TWO = 0.999
WEIGHT_DECAY = 0.01
ADAM_EPS = 1e-08

F32 = jnp.float32
BF16 = jnp.bfloat16
MESH = pl.DeviceIdType.MESH
NT = (((1,), (1,)), ((), ()))
NN = (((1,), (0,)), ((), ()))

WIDE = 3 * HID
HALL = 3 * WIDE
FEAT = 3 * CIN
FPAD = 256
KALL = HALL + FPAD
PARTS = [
    (0, 0, WIDE + FEAT, 512),
    (1, 0, WIDE + FEAT, 512),
    (2, 2 * HID, WIDE + FEAT, 256),
    (2, 0, 2 * HID, 256),
]
DIRECT = 3
SUB = 32
UNIT = 16


def sigmoid(v):
    return 0.5 * jnp.tanh(0.5 * v) + 0.5


def mm(a, b, dims):
    return lax.dot_general(a, b, dims, preferred_element_type=F32)


def layer_kernel(
    dims,
    crop_ref,
    frames_ref,
    kt_ref,
    bias_ref,
    peep_ref,
    cot_hbm,
    hid_hbm,
    fg_hbm,
    grad_ref,
    small_out,
    norm_out,
    wt,
    wft,
    fr,
    xt,
    xt0,
    sc,
    gates,
    cells,
    gpre,
    gs,
    cot,
    consts,
    sums,
    acc,
    fzero,
    fgo,
    fhalo_s,
    fhalo_r,
    shalo_r,
    ghalo_s,
    ghalo_r,
    bhalo_s,
    bhalo_r,
    nat,
    *rest,
):
    nbat, nrow, frames_n, rows_n, nfar, nmid, ncore, nlow = dims
    pix = rows_n * WID
    rest = list(rest)
    core_send, core_recv, mid_send, mid_recv, far_send, far_recv = (
        [rest.pop(0) for _ in PARTS] for _ in range(6)
    )
    small_bufs = [rest.pop(0) for _ in range(4)]
    tail_send, tail_recv = ([rest.pop(0) for _ in PARTS[DIRECT:]] for _ in range(2))
    low_send, low_recv = rest.pop(0), rest.pop(0)
    norm_tiles, nsems = rest.pop(0), rest.pop(0)
    sems = rest.pop(0)
    rsems = rest.pop(0)
    lsems = rest.pop(0)

    at_b = lax.axis_index("batch")
    at_r = lax.axis_index("rows")
    counter = [0]
    pending = []

    def remote(src, dst, bat, row):
        i = counter[0]
        counter[0] += 1
        c = pltpu.make_async_remote_copy(
            src_ref=src, dst_ref=dst, send_sem=sems.at[i], recv_sem=rsems.at[i],
            device_id=(bat, row), device_id_type=MESH,
        )
        c.start()
        pending.append(c)
        return c

    far, near = at_b // 2, at_b % 2
    low = at_r % nlow
    core = (at_r // nlow) % ncore
    half = nmid // 2
    mid = near * half + at_r // (nlow * ncore)

    def device(f, m, c, w):
        return (f * 2 + m // half, ((m % half) * ncore + c) * nlow + w)

    def far_peer(k):
        return device(lax.rem(far + k, nfar), mid, core, low)

    def mid_peer(k):
        return device(far, lax.rem(mid + k, nmid), core, low)

    def core_peer(k):
        return device(far, mid, lax.rem(core + k, ncore), low)

    def low_peer(k):
        return device(far, mid, core, lax.rem(low + k, nlow))

    groups = [(nfar, far_peer, far), (nmid, mid_peer, mid), (ncore, core_peer, core), (nlow, low_peer, low)]
    up_r = lax.rem(at_r + nrow - 1, nrow)
    down_r = lax.rem(at_r + 1, nrow)

    barrier = pltpu.get_barrier_semaphore()
    ndev = nbat * nrow
    me = at_b * nrow + at_r

    def any_peer(k):
        to = lax.rem(me + k, ndev)
        return (to // nrow, lax.rem(to, nrow))

    partners = [(at_b, up_r), (at_b, down_r)]
    partners += [peer(k) for size, peer, _ in groups for k in range(1, size)]
    for to in partners:
        pl.semaphore_signal(barrier, inc=1, device_id=to, device_id_type=MESH)

    cot_copy = pltpu.make_async_copy(cot_hbm.at[0], cot, lsems.at[0])
    cot_copy.start()

    ktv = kt_ref[...]
    own = []
    for tap in range(9):
        own.append(ktv[:, tap * (CIN + HID) + CIN : (tap + 1) * (CIN + HID)])
    for tap in range(9):
        own.append(ktv[:, tap * (CIN + HID) : tap * (CIN + HID) + CIN])
    own.append(jnp.zeros((UNIT, FPAD - 9 * CIN), F32))
    wt[far, mid, core] = jnp.concatenate(own, axis=1).astype(BF16)

    rows_own = GATES // (nbat * nrow)
    flat = (at_b * nrow + at_r) * rows_own
    peep_own = HID // nbat
    tile_row = lax.broadcasted_iota(jnp.int32, (8, HID), 0)
    consts[...] = jnp.zeros_like(consts)
    consts[0:3, 0:peep_own] = peep_ref[...]
    consts[4:5, 0:rows_own] = bias_ref[...]
    peep_tile = pltpu.roll(jnp.where(tile_row < 3, consts[...], 0.0), at_b * peep_own, 1)
    bias_tile = pltpu.roll(jnp.broadcast_to(consts[4:5, :], (8, HID)), flat % HID, 1)
    bias_tile = jnp.where(tile_row == 4 + flat // HID, bias_tile, 0.0)
    start_tile = jnp.where(at_r == 0, peep_tile, 0.0) + bias_tile

    small_step = [0] * 2
    small_moving = [None] * 2

    def small_next(i, tile=None):
        s = small_step[i]
        small_step[i] = s + 1
        while s < 4 and groups[s][0] == 1:
            s += 1
            small_step[i] = s + 1
        if tile is None:
            done = s - 1
            while groups[done][0] == 1:
                done -= 1
            for c in small_moving[i]:
                c.wait_recv()
            tile = small_bufs[done][i, 0]
            for k in range(1, groups[done][0]):
                tile = tile + small_bufs[done][i, k]
        if s < 4:
            size, peer, place = groups[s]
            ref = small_bufs[s].at[i, place]
            ref[...] = tile
            small_moving[i] = [remote(ref, ref, *peer(k)) for k in range(1, size)]
            return None
        return tile

    def small_finish(i):
        while True:
            tile = small_next(i)
            if tile is not None:
                return tile

    lanes = [(HALL, KALL), (0, WIDE), (WIDE, 2 * WIDE), (2 * WIDE, HALL)]
    steps = [0] * 4
    moving = [None] * 4

    def gather_low():
        if nlow > 1:
            low_send[...] = wt[far, mid, core]
            copies = [remote(low_send, low_recv.at[0, k - 1], *low_peer(k)) for k in range(1, nlow)]
            total = low_send[...]
            for k in range(1, nlow):
                copies[k - 1].wait_recv()
                total = total + low_recv[0, k - 1]
            wt[far, mid, core] = total

    def gather_step(i):
        lo, up = lanes[i]
        cols = pl.ds(lo, up - lo)
        s = steps[i]
        steps[i] = s + 1
        if 0 < s < 4:
            for c in moving[i]:
                c.wait_recv()
        if s < 3:
            g = (1, 0, 2)[s] if i == 1 else s
            size, peer, _ = groups[g]
            if s == 0:
                ref = wt.at[far, mid, core, :, cols]
            elif s == 1:
                ref = wt.at[far, :, core, :, cols] if i == 1 else wt.at[:, mid, core, :, cols]
            else:
                ref = wt.at[:, :, core, :, cols]
            moving[i] = [remote(ref, ref, *peer(k)) for k in range(1, size)]

    crop_h = crop_ref[0, 0]
    crop_w = crop_ref[0, 1]
    row0 = at_r * rows_n
    has_up = (at_r > 0).astype(F32)
    has_down = (at_r < nrow - 1).astype(F32)

    rr3 = lax.broadcasted_iota(jnp.int32, (CIN, rows_n, WID), 1) + row0
    cc3 = lax.broadcasted_iota(jnp.int32, (CIN, rows_n, WID), 2)
    live3 = (rr3 < crop_h) & (cc3 < crop_w)
    for t in range(frames_n):
        masked = jnp.where(live3, frames_ref[0, t].astype(F32), 0.0)
        fr[t, 1 : rows_n + 1] = jnp.swapaxes(masked, 0, 1)
        fhalo_s[0, t] = fr[t, 1].astype(BF16)
        fhalo_s[1, t] = fr[t, rows_n].astype(BF16)

    def lane_shift(v, by):
        at = lax.broadcasted_iota(jnp.int32, v.shape, 1)
        if by > 0:
            return jnp.where(at == WID - 1, 0.0, pltpu.roll(v, WID - 1, 1))
        return jnp.where(at == 0, 0.0, pltpu.roll(v, 1, 1))

    def row_shift(v, by):
        at = lax.broadcasted_iota(jnp.int32, v.shape, 0)
        if by > 0:
            return jnp.where(at == WID - 1, 0.0, pltpu.roll(v, WID - 1, 0))
        return jnp.where(at == 0, 0.0, pltpu.roll(v, 1, 0))

    def frame_part(t):
        return xt.at[t - 1, WIDE : WIDE + FEAT] if t > 0 else xt0

    def frame_cols(t, rr):
        v = fr[t, rr]
        three = jnp.concatenate([lane_shift(v, -1), v, lane_shift(v, 1)], axis=0)
        frame_part(t)[:, pl.ds(pl.multiple_of(rr * WID, WID), WID)] = three.astype(BF16)

    def frame_cols_all(rr, carry):
        for t in range(frames_n):
            frame_cols(t, rr)
        return carry

    def frame_pixels(t, lo, up):
        def one(rr, carry):
            parts = [
                frame_part(t)[:, pl.ds(pl.multiple_of((rr + a) * WID, WID), WID)].astype(F32)
                for a in range(3)
            ]
            parts.append(jnp.zeros((FPAD - 9 * CIN, WID), F32))
            gpre[t, pl.ds(pl.multiple_of(rr * WID, WID), WID), 0:FPAD] = (
                jnp.concatenate(parts, axis=0).T.astype(BF16)
            )
            return carry

        lax.fori_loop(lo, up, one, 0)

    lax.fori_loop(1, rows_n + 1, frame_cols_all, 0)
    frame_pixels(0, 1, rows_n - 1)

    pl.semaphore_wait(barrier, len(partners))
    gather_low()
    gather_step(0)
    gather_step(1)
    small_next(0, start_tile)
    f_up = remote(fhalo_s.at[0], fhalo_r.at[1], at_b, up_r)
    f_down = remote(fhalo_s.at[1], fhalo_r.at[0], at_b, down_r)
    gather_step(2)
    gather_step(3)
    if frames_n > 1:
        frame_pixels(1, 1, rows_n - 1)
    f_up.wait_recv()
    f_down.wait_recv()
    for t in range(frames_n):
        fr[t, 0] = fhalo_r[0, t].astype(F32) * has_up
        fr[t, rows_n + 1] = fhalo_r[1, t].astype(F32) * has_down
        frame_cols(t, 0)
        frame_cols(t, rows_n + 1)
    gather_step(1)
    gather_step(0)
    small_next(0)
    gather_step(2)
    for t in range(min(2, frames_n)):
        frame_pixels(t, 0, 1)
        frame_pixels(t, rows_n - 1, rows_n)
    gather_step(3)
    if frames_n > 2:
        frame_pixels(2, 0, rows_n)
    gather_step(0)
    small_next(0)
    for t in range(3, frames_n):
        frame_pixels(t, 0, rows_n)
    gather_step(0)

    consts[...] = small_finish(0)
    peep = [consts[i : i + 1, :] for i in range(3)]
    bias = [consts[4 + i : 5 + i, :] for i in range(4)]

    def cat_wt(lo, up):
        return wt[:, :, :, :, lo:up].reshape(GATES, up - lo)

    sub_iota = lax.broadcasted_iota(jnp.int32, (SUB, HID), 0)

    def live_cols(rr):
        return jnp.where(row0 + rr < crop_h, crop_w, 0)

    def place_state(t, v, at):
        three = [row_shift(v, -1), v, row_shift(v, 1)]
        for j in range(3):
            low_j = three[j].astype(BF16)
            sc[t, at, :, j * HID : (j + 1) * HID] = low_j
            xt[t, j * HID : (j + 1) * HID, at * WID : (at + 1) * WID] = low_j.T

    CH = 4
    nchunk = rows_n // CH

    def forward_dot(t, m):
        px = pl.ds(m * CH * WID, CH * WID)
        xf = gpre[t, px, 0:FPAD]
        if t > 0:
            parts = [sc[t - 1, m * CH + a : m * CH + a + CH].reshape(CH * WID, WIDE) for a in range(3)]
            x = jnp.concatenate(parts + [xf], axis=1)
            gates[t, px, :] = mm(x, cat_wt(0, KALL), NT)
        else:
            gates[t, px, :] = mm(xf, cat_wt(HALL, KALL), NT)

    def forward_rows(t, m):
        for rr in range(m * CH, (m + 1) * CH):
            limit = live_cols(rr)
            state = []
            for j in range(WID // SUB):
                sl = pl.ds(rr * WID + j * SUB, SUB)
                live = sub_iota + j * SUB < limit
                zi = gates[t, sl, 0:HID] + bias[0]
                zc = gates[t, sl, 2 * HID : 3 * HID] + bias[2]
                zo = gates[t, sl, 3 * HID :] + bias[3]
                if t > 0:
                    prev = cells[t - 1, sl, :]
                    zf = gates[t, sl, HID : 2 * HID] + bias[1] + peep[1] * prev
                    zi = zi + peep[0] * prev
                    gf = sigmoid(zf)
                    gates[t, sl, HID : 2 * HID] = gf
                gi = sigmoid(zi)
                gc = jnp.tanh(zc)
                c = gi * gc
                if t > 0:
                    c = c + gf * prev
                c = jnp.where(live, c, 0.0)
                go = sigmoid(zo + peep[2] * c)
                gates[t, sl, 0:HID] = gi
                gates[t, sl, 2 * HID : 3 * HID] = gc
                gates[t, sl, 3 * HID :] = go
                cells[t, sl, :] = c
                state.append(jnp.where(live, go * jnp.tanh(c), 0.0))
            state = jnp.concatenate(state, axis=0)
            if t < frames_n - 1:
                place_state(t, state, rr + 1)
            else:
                sc[0, rr + 1, :, 0:HID] = state.astype(BF16)

    hid_copies = []
    center = pl.ds(HID, HID)
    halos = [[None, None] for _ in range(frames_n)]

    def state_done(t, m):
        if t < frames_n - 1 and m == 0:
            halos[t][1] = remote(sc.at[t, 1, :, center], shalo_r.at[t, 1], at_b, up_r)
        if t < frames_n - 1 and m == nchunk - 1:
            halos[t][0] = remote(sc.at[t, rows_n, :, center], shalo_r.at[t, 0], at_b, down_r)
        if (t, m) == last_of[t]:
            lanes_of = center if t < frames_n - 1 else pl.ds(0, HID)
            src = sc.at[t if t < frames_n - 1 else 0, pl.ds(1, rows_n), :, lanes_of]
            c = pltpu.make_async_copy(src, hid_hbm.at[0, t], lsems.at[1 + t])
            c.start()
            hid_copies.append(c)

    inner = list(range(1, nchunk - 1))
    order = [inner + [nchunk - 1, 0], inner[::-1] + [0, nchunk - 1]]
    slots = [(0, m) for m in range(nchunk)] + [(t, m) for t in range(1, frames_n) for m in order[(t + 1) % 2]]
    last_of = {t: [s for s in slots if s[0] == t][-1] for t in range(frames_n)}
    for i, (t, m) in enumerate(slots + [(frames_n, 0)]):
        if t == 1 and m == order[0][0]:
            for k in range(1, 4):
                while steps[k] < 4:
                    gather_step(k)
        if 0 < t < frames_n and m == 0:
            halos[t - 1][0].wait_recv()
            place_state(t - 1, shalo_r[t - 1, 0].astype(F32) * has_up, 0)
        if 0 < t < frames_n and m == nchunk - 1:
            halos[t - 1][1].wait_recv()
            place_state(t - 1, shalo_r[t - 1, 1].astype(F32) * has_down, rows_n + 1)
        if t < frames_n:
            forward_dot(t, m)
        if i > 0:
            forward_rows(*slots[i - 1])
            state_done(*slots[i - 1])
        if t == 0 and 0 < m < 4:
            gather_step(m)

    cot_copy.wait()
    sums[...] = jnp.zeros_like(sums)

    def fold(v):
        return jnp.sum(v.reshape(SUB // 8, 8, HID), axis=0)

    def backward_rows(t, m):
        parts = [None] * 7
        for rr in range(m * CH, (m + 1) * CH):
            limit = live_cols(rr)
            for j in range(WID // SUB):
                cols = slice(j * SUB, (j + 1) * SUB)
                sl = pl.ds(rr * WID + j * SUB, SUB)
                live = sub_iota + j * SUB < limit
                gi = gates[t, sl, 0:HID]
                gc = gates[t, sl, 2 * HID : 3 * HID]
                go = gates[t, sl, 3 * HID :]
                c = cells[t, sl, :]
                sq = jnp.tanh(c)
                total = cot[t, rr, cols, :].astype(F32)
                if t < frames_n - 1:
                    total = total + gs[(t + 1) % 2, rr + 1, cols, :]
                    if rr == 0:
                        total = total + ghalo_r[t, 0, cols, :].astype(F32) * has_up
                    if rr == rows_n - 1:
                        total = total + ghalo_r[t, 1, cols, :].astype(F32) * has_down
                total = jnp.where(live, total, 0.0)
                tgo = total * go
                d_out = tgo * sq * (1.0 - go)
                nxt = tgo * (1.0 - sq * sq) + peep[2] * d_out
                if t < frames_n - 1:
                    nxt = nxt + cells[t + 1, sl, :]
                kept = jnp.where(live, nxt, 0.0)
                kgi = kept * gi
                d_in = kgi * gc * (1.0 - gi)
                d_cand = kgi * (1.0 - gc * gc)
                vals = [d_in, None, d_cand, d_out, None, None, d_out * c]
                if t > 0:
                    gf = gates[t, sl, HID : 2 * HID]
                    prev = cells[t - 1, sl, :]
                    kgf = kept * gf
                    d_for = kgf * prev * (1.0 - gf)
                    cells[t, sl, :] = kgf + peep[0] * d_in + peep[1] * d_for
                    vals[1] = d_for
                    vals[4] = d_in * prev
                    vals[5] = d_for * prev
                gpre[t, sl, 0:HID] = d_in.astype(BF16)
                gpre[t, sl, HID : 2 * HID] = (vals[1] if t > 0 else jnp.zeros_like(d_in)).astype(BF16)
                gpre[t, sl, 2 * HID : 3 * HID] = d_cand.astype(BF16)
                gpre[t, sl, 3 * HID :] = d_out.astype(BF16)
                for i in range(7):
                    if vals[i] is not None:
                        f = fold(vals[i])
                        parts[i] = f if parts[i] is None else parts[i] + f
        for i in range(7):
            if parts[i] is not None:
                sums[i] = sums[i] + parts[i]

    def state_chunk(t, m, done):
        y = mm(gpre[t, m * CH * WID : (m + 1) * CH * WID, :], cat_wt(0, HALL), NN)
        row = [None] * (CH + 2)
        for i in range(CH):
            for a in range(3):
                three = [y[i * WID : (i + 1) * WID, a * WIDE + j * HID : a * WIDE + (j + 1) * HID] for j in range(3)]
                z = three[1] + row_shift(three[0], 1) + row_shift(three[2], -1)
                row[i + a] = z if row[i + a] is None else row[i + a] + z
        for k in range(CH + 2):
            at = m * CH + k
            gs[t % 2, at] = gs[t % 2, at] + row[k] if at in done else row[k]
            done.add(at)

    work = [(t, m) for t in reversed(range(frames_n)) for m in order[(frames_n - 1 - t) % 2]]
    backward_rows(*work[0])
    ghalos = [[None, None] for _ in range(frames_n)]

    def rows_ready(t, m):
        if t < frames_n - 1 and m in (0, nchunk - 1):
            ghalos[t + 1][0 if m == 0 else 1].wait_recv()

    written = {t: set() for t in range(frames_n)}
    for i, (t, m) in enumerate(work):
        if t == 0:
            break
        rows_ready(*work[i + 1])
        state_chunk(t, m, written[t])
        backward_rows(*work[i + 1])
        if m == 0:
            ghalo_s[t - 1, 0] = gs[t % 2, 0].astype(BF16)
            ghalos[t][1] = remote(ghalo_s.at[t - 1, 0], ghalo_r.at[t - 1, 1], at_b, up_r)
        if m == nchunk - 1:
            ghalo_s[t - 1, 1] = gs[t % 2, rows_n + 1].astype(BF16)
            ghalos[t][0] = remote(ghalo_s.at[t - 1, 1], ghalo_r.at[t - 1, 0], at_b, down_r)
    left = work[-(nchunk - 1) :]

    stage = [0] * 4
    flight = [None] * 4
    last = len(PARTS) - 1
    def reduce_step(q):
        s = stage[q]
        stage[q] = s + 1
        first = acc[q][0]
        second = acc[q][1] if ncore > 1 else first.at[:, :, 0]
        if s == 0 and ncore > 1:
            core_send[q][...] = first[:, :, 1 - core].astype(BF16)
            flight[q] = [remote(core_send[q], core_recv[q], *core_peer(1))]
        elif s == 1:
            if ncore > 1:
                flight[q][0].wait_recv()
                second[...] = first[:, :, core] + core_recv[q][...].astype(F32)
            flight[q] = []
            if q >= DIRECT:
                tail_send[q - DIRECT][...] = second[...].astype(BF16)
                for k in range(1, nfar * nmid):
                    to = lax.rem(far * nmid + mid + k, nfar * nmid)
                    src = tail_send[q - DIRECT].at[to // nmid, to % nmid]
                    flight[q].append(remote(src, tail_recv[q - DIRECT].at[k - 1], *device(to // nmid, to % nmid, core, low)))
                return
            for k in range(1, nmid):
                to = lax.rem(mid + k, nmid)
                mid_send[q][k - 1] = second[:, to].astype(BF16)
                flight[q].append(remote(mid_send[q].at[k - 1], mid_recv[q].at[k - 1], *mid_peer(k)))
        elif s == 2 and q < DIRECT:
            total = second[:, mid]
            for k in range(1, nmid):
                flight[q][k - 1].wait_recv()
                total = total + mid_recv[q][k - 1].astype(F32)
            second[:, mid] = total
            far_send[q][...] = total.astype(BF16)
            flight[q] = []
            for k in range(1, nfar):
                to = lax.rem(far + k, nfar)
                flight[q].append(remote(far_send[q].at[to], far_recv[q].at[k - 1], *far_peer(k)))
        elif s == 3 or s == 2:
            stage[q] = 4
            total = second[far, mid]
            arrived = tail_recv[q - DIRECT] if q >= DIRECT else far_recv[q]
            for k in range(len(flight[q])):
                flight[q][k].wait_recv()
                total = total + arrived[k].astype(F32)
            a, lo, up, _ = PARTS[q]
            for j in range(3):
                at = (3 * a + j) * (CIN + HID)
                if up > WIDE:
                    nat[:, at : at + CIN] = total[:, WIDE - lo + j * CIN : WIDE - lo + (j + 1) * CIN]
                if lo <= j * HID < up:
                    nat[:, at + CIN : at + CIN + HID] = total[:, j * HID - lo : (j + 1) * HID - lo]

    def kernel_dot(q, t):
        a, lo, up, _ = PARTS[q]
        return mm(xt[t - 1, lo:up, a * WID : a * WID + pix], gpre[t], NN)

    def finish_rows(k):
        rows_ready(*left[k])
        backward_rows(*left[k])

    def place_part(q, total):
        a, lo, up, wide = PARTS[q]
        pieces = [total]
        if up > WIDE:
            pieces = [total[: WIDE - lo], total[WIDE - lo :] + fzero[a * FEAT : (a + 1) * FEAT, :]]
        if wide > up - lo:
            pieces.append(jnp.zeros((wide - up + lo, GATES), F32))
        acc[q][0][...] = jnp.concatenate(pieces, axis=0).T.reshape(acc[q][0].shape)

    after = {(1, 1): [0], (1, 2): [0], (2, 1): [1], (2, 2): [1], (3, 1): [2], (3, 2): [2]}
    totals = [None] * 4
    for q in range(4):
        for t in range(1, frames_n):
            part = kernel_dot(q, t)
            totals[q] = part if t == 1 else totals[q] + part
            if q == 0 and t - 1 < len(left):
                finish_rows(t - 1)
            if q > 0 and t == 1:
                place_part(q - 1, totals[q - 1])
            for k in after.get((q, t), []):
                reduce_step(k)
        if q == 0:
            for k in range(frames_n - 1, len(left)):
                finish_rows(k)
            g0 = [xt0[:, k * WID : k * WID + pix] for k in range(3)]
            fzero[...] = mm(jnp.concatenate(g0, axis=0), gpre[0], NN)
            rows = [jnp.sum(sums[i], axis=0, keepdims=True) for i in range(7)]
            small_next(1, jnp.concatenate(rows[4:] + [jnp.zeros((1, HID), F32)] + rows[:4], axis=0))
        elif q < 3:
            small_next(1)
    place_part(last, totals[last])
    reduce_step(last)
    reduce_step(0)

    fgb = fr

    def frame_back(t):
        y = mm(wft[0 : 9 * CIN, :], gpre[t], NT)
        row = [None] * (rows_n + 2)
        for i in range(rows_n):
            for a in range(3):
                part = y[a * FEAT : (a + 1) * FEAT, i * WID : (i + 1) * WID]
                z = part[CIN : 2 * CIN] + lane_shift(part[0:CIN], 1) + lane_shift(part[2 * CIN :], -1)
                row[i + a] = z if row[i + a] is None else row[i + a] + z
        for at in range(rows_n + 2):
            fgb[t, at] = row[at]
        bhalo_s[0, t] = row[0].astype(BF16)
        bhalo_s[1, t] = row[rows_n + 1].astype(BF16)

    wft[...] = cat_wt(HALL, KALL).astype(F32).T.astype(BF16)
    between = [[last], [], [1], [2]]
    for t in range(frames_n):
        frame_back(t)
        for q in between[t] if t < 4 else []:
            reduce_step(q)
    f_up = remote(bhalo_s.at[0], bhalo_r.at[1], at_b, up_r)
    f_down = remote(bhalo_s.at[1], bhalo_r.at[0], at_b, down_r)
    for q in (0, 3, 1, 2):
        while stage[q] < 4:
            reduce_step(q)
    if nlow > 1:
        low_send[...] = nat[...].astype(BF16)
        copies = [remote(low_send, low_recv.at[1, k - 1], *low_peer(k)) for k in range(1, nlow)]
        total = nat[...]
        for k in range(1, nlow):
            copies[k - 1].wait_recv()
            total = total + low_recv[1, k - 1].astype(F32)
        nat[...] = total

    g = nat[:, 0:KROWS]
    squares = g * g
    if nlow > 1:
        base = low * rows_own
        ri = lax.broadcasted_iota(jnp.int32, squares.shape, 0)
        squares = jnp.where((ri >= base) & (ri < base + rows_own), squares, 0.0)
    norm_tiles[me] = jnp.broadcast_to(jnp.sum(squares), (8, HID))

    def norm_copy(k):
        row = norm_tiles.at[me, 0:1]
        return pltpu.make_async_remote_copy(
            src_ref=row, dst_ref=row, send_sem=nsems.at[0, k], recv_sem=nsems.at[1, k],
            device_id=any_peer(k), device_id_type=MESH,
        )

    lax.fori_loop(1, ndev, lambda k, c: (norm_copy(k).start(), c)[1], 0)
    grad_ref[...] = g
    small = small_finish(1)
    small_out[...] = small
    f_up.wait_recv()
    f_down.wait_recv()
    for t in range(frames_n):
        fgb[t, 1] = fgb[t, 1] + bhalo_r[0, t].astype(F32) * has_up
        fgb[t, rows_n] = fgb[t, rows_n] + bhalo_r[1, t].astype(F32) * has_down
        fgo[t] = jnp.where(live3, jnp.swapaxes(fgb[t, 1 : rows_n + 1], 0, 1), 0.0)
    c = pltpu.make_async_copy(fgo, fg_hbm.at[0], lsems.at[1 + frames_n])
    c.start()
    hid_copies.append(c)
    lax.fori_loop(1, ndev, lambda k, c: (norm_copy(k).wait_recv(), c)[1], 0)
    squares = jnp.sum(norm_tiles[:, 0:1, :], axis=0) + jnp.sum(small * small)
    norm_out[...] = jnp.broadcast_to(jnp.sqrt(squares), (8, HID))
    lax.fori_loop(1, ndev, lambda k, c: (norm_copy(k).wait_send(), c)[1], 0)

    for c in hid_copies:
        c.wait()
    for c in pending:
        c.wait_send()


def adamw_update(weight, gradient, first, second, scale):
    clipped = gradient * scale
    first_new = BETA_ONE * first + (1.0 - BETA_ONE) * clipped
    second_new = BETA_TWO * second + (1.0 - BETA_TWO) * clipped * clipped
    first_hat = first_new / (1.0 - BETA_ONE**STEP)
    second_hat = second_new / (1.0 - BETA_TWO**STEP)
    weight_new = weight - LEARN_RATE * (
        first_hat / (jnp.sqrt(second_hat) + ADAM_EPS) + WEIGHT_DECAY * weight
    )
    return (weight_new, first_new, second_new)


def update_kernel(
    dims, hid_in, fg_in, norm_ref, sum_ref, small_ref,
    k_ref, b_ref, p_ref, k1_ref, k2_ref, b1_ref, b2_ref, p1_ref, p2_ref,
    hid_out, fg_out, norm_out, ko, k1o, k2o, bo, b1o, b2o, po, p1o, p2o, hid_buf, fg_buf, sems,
):
    nbat, nrow = dims
    frames_n = hid_buf.shape[0]
    fetch, put = [], []
    for t in range(frames_n):
        for i, (src, buf, dst) in enumerate(((hid_in, hid_buf, hid_out), (fg_in, fg_buf, fg_out))):
            fetch.append(pltpu.make_async_copy(src.at[0, t], buf.at[t], sems.at[i, t]))
            put.append(pltpu.make_async_copy(buf.at[t], dst.at[0, t], sems.at[2 + i, t]))
    for c in fetch:
        c.start()
    at_b = lax.axis_index("batch")
    at_r = lax.axis_index("rows")
    norm_out[0, 0] = norm_ref[0, 0]
    norm = jnp.full((1, HID), norm_ref[0, 0], F32)
    scale = jnp.minimum(1.0, CLIP_AT / (norm + 1e-06))
    small = small_ref[...]
    rows_own = b_ref.shape[1]
    peep_own = p_ref.shape[1]
    flat = (at_b * nrow + at_r) * rows_own
    lane_back = lax.rem(HID - flat % HID, HID)
    tile_row = lax.broadcasted_iota(jnp.int32, (8, HID), 0)
    picked = jnp.where(tile_row == 4 + flat // HID, small, 0.0)
    picked = jnp.sum(pltpu.roll(picked, lane_back, 1), axis=0, keepdims=True)
    new = adamw_update(b_ref[...], picked[:, 0:rows_own], b1_ref[...], b2_ref[...], scale[:, 0:rows_own])
    bo[...], b1o[...], b2o[...] = new
    shifted = pltpu.roll(small, lax.rem(HID - at_b * peep_own, HID), 1)
    new = adamw_update(p_ref[...], shifted[0:3, 0:peep_own], p1_ref[...], p2_ref[...], scale[:, 0:peep_own])
    po[...], p1o[...], p2o[...] = new
    new = adamw_update(k_ref[...], sum_ref[...], k1_ref[...], k2_ref[...], scale[:, 0:1])
    ko[...], k1o[...], k2o[...] = new
    for i in range(len(fetch)):
        fetch[i].wait()
        put[i].start()
    for c in put:
        c.wait()


def local(
    nbat,
    nrow,
    frames,
    crop_sizes,
    kernel,
    gate_bias,
    peepholes,
    cotangent,
    kernel_first,
    kernel_second,
    bias_first,
    bias_second,
    peep_first,
    peep_second,
):
    frames_n, rows_n = frames.shape[1], frames.shape[3]
    pix = rows_n * WID
    own = kernel.shape[1]
    nlow = max(1, UNIT // own)
    ncore = 2 if nrow > nlow else 1
    nmid = 2 * (nrow // (nlow * ncore))
    nfar = nbat // 2
    at_r = lax.axis_index("rows")

    kt = kernel.T
    if nlow > 1:
        kt = lax.dynamic_update_slice(
            jnp.zeros((UNIT, KROWS), F32), kt, (lax.rem(at_r, nlow) * own, 0)
        )
    bias_row = gate_bias.reshape(1, own)

    vm = pltpu.VMEM
    pair = (nfar, nmid) if ncore > 1 else (1, 1)
    wides = [(UNIT, part[3]) for part in PARTS]
    acc_shapes = [[vm((nfar, nmid, ncore) + wide, F32), vm(pair + wide, F32)] for wide in wides]
    ncopies = (
        2 * (nfar + nmid + ncore + nlow - 4)
        + 4 * (nfar + nmid + ncore - 3)
        + DIRECT * (nfar + nmid - 2)
        + len(PARTS) * (ncore - 1)
        + (len(PARTS) - DIRECT) * (nfar * nmid - 1)
        + 4
        + 4 * (frames_n - 1)
        + 2 * (nlow - 1)
    )
    scratch = [
        vm((nfar, nmid, ncore, UNIT, KALL), BF16),
        vm((FPAD, GATES), BF16),
        vm((frames_n, rows_n + 2, CIN, WID), F32),
        vm((frames_n - 1, WIDE + FEAT, (rows_n + 2) * WID), BF16),
        vm((FEAT, (rows_n + 2) * WID), BF16),
        vm((frames_n - 1, rows_n + 2, WID, WIDE), BF16),
        vm((frames_n, pix, GATES), F32),
        vm((frames_n, pix, HID), F32),
        vm((frames_n, pix, GATES), BF16),
        vm((2, rows_n + 2, WID, HID), F32),
        vm((frames_n, rows_n, WID, HID), BF16),
        vm((8, HID), F32),
        vm((7, 8, HID), F32),
        acc_shapes,
        vm((9 * CIN, GATES), F32),
        vm((frames_n, CIN, rows_n, WID), F32),
        vm((2, frames_n, CIN, WID), BF16),
        vm((2, frames_n, CIN, WID), BF16),
        vm((frames_n - 1, 2, WID, HID), BF16),
        vm((frames_n - 1, 2, WID, HID), BF16),
        vm((frames_n - 1, 2, WID, HID), BF16),
        vm((2, frames_n, CIN, WID), BF16),
        vm((2, frames_n, CIN, WID), BF16),
        vm((UNIT, KALL), F32),
    ]
    scratch += [vm(pair + wide, BF16) for wide in wides + wides]
    two = [wide if q < DIRECT else (8, HID) for q, wide in enumerate(wides)]
    mids = [(nmid - 1, nfar) if q < DIRECT else (1, 1) for q in range(len(two))]
    fars = [(nfar,) if q < DIRECT else (1,) for q in range(len(two))]
    scratch += [vm(mids[q] + two[q], BF16) for q in range(len(two))] * 2
    scratch += [vm(fars[q] + two[q], BF16) for q in range(len(two))] * 2
    scratch += [vm((2, size, 8, HID), F32) for size in (nfar, nmid, ncore, nlow)]
    scratch += [vm((nfar, nmid) + wide, BF16) for wide in wides[DIRECT:]]
    scratch += [vm((nfar * nmid - 1,) + wide, BF16) for wide in wides[DIRECT:]]
    scratch += [vm((UNIT, KALL), BF16), vm((2, max(1, nlow - 1), UNIT, KALL), BF16)]
    scratch += [vm((nbat * nrow, 8, HID), F32), pltpu.SemaphoreType.DMA((2, nbat * nrow))]
    scratch += [
        pltpu.SemaphoreType.DMA((ncopies,)),
        pltpu.SemaphoreType.DMA((ncopies,)),
        pltpu.SemaphoreType.DMA((2 + frames_n,)),
    ]
    smem = pl.BlockSpec(memory_space=pltpu.SMEM)
    vmem = pl.BlockSpec(memory_space=pltpu.VMEM)
    hbm = pl.BlockSpec(memory_space=pl.ANY)
    dims = (nbat, nrow, frames_n, rows_n, nfar, nmid, ncore, nlow)
    hidden, frames_back, kernel_sum, small_sum, norm = pl.pallas_call(
        functools.partial(layer_kernel, dims),
        out_shape=(
            jax.ShapeDtypeStruct(cotangent.shape, BF16),
            jax.ShapeDtypeStruct(frames.shape, F32),
            jax.ShapeDtypeStruct((UNIT, KROWS), F32),
            jax.ShapeDtypeStruct((8, HID), F32),
            jax.ShapeDtypeStruct((8, HID), F32),
        ),
        in_specs=[smem, vmem, vmem, vmem, vmem, hbm],
        out_specs=(hbm, hbm, vmem, vmem, vmem),
        scratch_shapes=scratch,
        compiler_params=pltpu.CompilerParams(
            collective_id=0, has_side_effects=True, vmem_limit_bytes=63 << 20
        ),
        name="layer",
    )(crop_sizes, frames, kt, bias_row, peepholes, cotangent)

    if nlow > 1:
        kernel_sum = lax.dynamic_slice_in_dim(kernel_sum, lax.rem(at_r, nlow) * own, own, 0)
    kshape = jax.ShapeDtypeStruct((own, KROWS), F32)
    bshape = jax.ShapeDtypeStruct((1, own), F32)
    pshape = jax.ShapeDtypeStruct(peepholes.shape, F32)
    outs = pl.pallas_call(
        functools.partial(update_kernel, (nbat, nrow)),
        out_shape=(
            jax.ShapeDtypeStruct(cotangent.shape, BF16),
            jax.ShapeDtypeStruct(frames.shape, F32),
            jax.ShapeDtypeStruct((1, 1), F32),
        )
        + (kshape,) * 3 + (bshape,) * 3 + (pshape,) * 3,
        in_specs=[hbm, hbm, smem] + [vmem] * 11,
        out_specs=(hbm, hbm, smem) + (vmem,) * 9,
        scratch_shapes=[
            pltpu.VMEM(cotangent.shape[1:], BF16),
            pltpu.VMEM(frames.shape[1:], F32),
            pltpu.SemaphoreType.DMA((4, frames_n)),
        ],
        compiler_params=pltpu.CompilerParams(vmem_limit_bytes=63 << 20),
        name="update",
    )(
        hidden, frames_back, norm, kernel_sum, small_sum,
        kernel.T, bias_row, peepholes, kernel_first.T, kernel_second.T,
        bias_first.reshape(1, own), bias_second.reshape(1, own), peep_first, peep_second,
    )
    hidden_seq, frames_grad, norm = outs[:3]
    kernels, biases, peeps = outs[3:6], outs[6:9], outs[9:]
    return (
        hidden_seq,
        frames_grad,
        norm[0, 0],
        *(k.T for k in kernels),
        *(v.reshape(own) for v in biases),
        *peeps,
    )


def solution(mesh):
    return jax.shard_map(
        functools.partial(local, mesh.shape["batch"], mesh.shape["rows"]),
        mesh=mesh,
        in_specs=(
            P("batch", None, None, "rows", None),
            P("batch", None),
            P(None, ("batch", "rows")),
            P(("batch", "rows")),
            P(None, "batch"),
            P("batch", None, "rows", None, None),
            P(None, ("batch", "rows")),
            P(None, ("batch", "rows")),
            P(("batch", "rows")),
            P(("batch", "rows")),
            P(None, "batch"),
            P(None, "batch"),
        ),
        out_specs=(
            P("batch", None, "rows", None, None),
            P("batch", None, None, "rows", None),
            P(),
            P(None, ("batch", "rows")),
            P(None, ("batch", "rows")),
            P(None, ("batch", "rows")),
            P(("batch", "rows")),
            P(("batch", "rows")),
            P(("batch", "rows")),
            P(None, "batch"),
            P(None, "batch"),
            P(None, "batch"),
        ),
        check_vma=False,
    )
```

```python
import functools

import jax
import jax.numpy as jnp
from jax import lax
from jax.experimental import pallas as pl
from jax.experimental.pallas import tpu as pltpu
from jax.sharding import PartitionSpec as P

CIN = 16
HID = 128
GATES = 512
KROWS = 1296
WID = 128
STEP = 5
CLIP_AT = 0.02
LEARN_RATE = 0.02
BETA_ONE = 0.9
BETA_TWO = 0.999
WEIGHT_DECAY = 0.01
ADAM_EPS = 1e-08

F32 = jnp.float32
BF16 = jnp.bfloat16
MESH = pl.DeviceIdType.MESH
NT = (((1,), (1,)), ((), ()))
NN = (((1,), (0,)), ((), ()))

WIDE = 3 * HID
HALL = 3 * WIDE
FEAT = 3 * CIN
FPAD = 256
KALL = HALL + FPAD
PARTS = [
    (0, 0, WIDE + FEAT, 512),
    (1, 0, WIDE + FEAT, 512),
    (2, 2 * HID, WIDE + FEAT, 256),
    (2, 0, 2 * HID, 256),
]
DIRECT = 3
SUB = 32
UNIT = 16


def sigmoid(v):
    return 0.5 * jnp.tanh(0.5 * v) + 0.5


def mm(a, b, dims):
    return lax.dot_general(a, b, dims, preferred_element_type=F32)


def layer_kernel(
    dims,
    crop_ref,
    frames_ref,
    kt_ref,
    bias_ref,
    peep_ref,
    cot_hbm,
    hid_hbm,
    fg_hbm,
    grad_ref,
    small_out,
    norm_out,
    wt,
    wft,
    fr,
    xt,
    xt0,
    sc,
    gates,
    cells,
    gpre,
    gs,
    cot,
    consts,
    sums,
    acc,
    fzero,
    fgo,
    fhalo_s,
    fhalo_r,
    shalo_r,
    ghalo_s,
    ghalo_r,
    bhalo_s,
    bhalo_r,
    nat,
    *rest,
):
    nbat, nrow, frames_n, rows_n, nfar, nmid, ncore, nlow = dims
    pix = rows_n * WID
    rest = list(rest)
    core_send, core_recv, mid_send, mid_recv, far_send, far_recv = (
        [rest.pop(0) for _ in PARTS] for _ in range(6)
    )
    small_bufs = [rest.pop(0) for _ in range(4)]
    tail_send, tail_recv = ([rest.pop(0) for _ in PARTS[DIRECT:]] for _ in range(2))
    low_send, low_recv = rest.pop(0), rest.pop(0)
    norm_tiles, nsems = rest.pop(0), rest.pop(0)
    sems = rest.pop(0)
    rsems = rest.pop(0)
    lsems = rest.pop(0)

    at_b = lax.axis_index("batch")
    at_r = lax.axis_index("rows")
    counter = [0]
    pending = []

    def remote(src, dst, bat, row):
        i = counter[0]
        counter[0] += 1
        c = pltpu.make_async_remote_copy(
            src_ref=src, dst_ref=dst, send_sem=sems.at[i], recv_sem=rsems.at[i],
            device_id=(bat, row), device_id_type=MESH,
        )
        c.start()
        pending.append(c)
        return c

    far, near = at_b // 2, at_b % 2
    low = at_r % nlow
    core = (at_r // nlow) % ncore
    half = nmid // 2
    mid = near * half + at_r // (nlow * ncore)

    def device(f, m, c, w):
        return (f * 2 + m // half, ((m % half) * ncore + c) * nlow + w)

    def far_peer(k):
        return device(lax.rem(far + k, nfar), mid, core, low)

    def mid_peer(k):
        return device(far, lax.rem(mid + k, nmid), core, low)

    def core_peer(k):
        return device(far, mid, lax.rem(core + k, ncore), low)

    def low_peer(k):
        return device(far, mid, core, lax.rem(low + k, nlow))

    groups = [(nfar, far_peer, far), (nmid, mid_peer, mid), (ncore, core_peer, core), (nlow, low_peer, low)]
    up_r = lax.rem(at_r + nrow - 1, nrow)
    down_r = lax.rem(at_r + 1, nrow)

    barrier = pltpu.get_barrier_semaphore()
    ndev = nbat * nrow
    me = at_b * nrow + at_r

    def any_peer(k):
        to = lax.rem(me + k, ndev)
        return (to // nrow, lax.rem(to, nrow))

    partners = [(at_b, up_r), (at_b, down_r)]
    partners += [peer(k) for size, peer, _ in groups for k in range(1, size)]
    for to in partners:
        pl.semaphore_signal(barrier, inc=1, device_id=to, device_id_type=MESH)

    cot_copy = pltpu.make_async_copy(cot_hbm.at[0], cot, lsems.at[0])
    cot_copy.start()

    ktv = kt_ref[...]
    own = []
    for tap in range(9):
        own.append(ktv[:, tap * (CIN + HID) + CIN : (tap + 1) * (CIN + HID)])
    for tap in range(9):
        own.append(ktv[:, tap * (CIN + HID) : tap * (CIN + HID) + CIN])
    own.append(jnp.zeros((UNIT, FPAD - 9 * CIN), F32))
    wt[far, mid, core] = jnp.concatenate(own, axis=1).astype(BF16)

    rows_own = GATES // (nbat * nrow)
    flat = (at_b * nrow + at_r) * rows_own
    peep_own = HID // nbat
    tile_row = lax.broadcasted_iota(jnp.int32, (8, HID), 0)
    consts[...] = jnp.zeros_like(consts)
    consts[0:3, 0:peep_own] = peep_ref[...]
    consts[4:5, 0:rows_own] = bias_ref[...]
    peep_tile = pltpu.roll(jnp.where(tile_row < 3, consts[...], 0.0), at_b * peep_own, 1)
    bias_tile = pltpu.roll(jnp.broadcast_to(consts[4:5, :], (8, HID)), flat % HID, 1)
    bias_tile = jnp.where(tile_row == 4 + flat // HID, bias_tile, 0.0)
    start_tile = jnp.where(at_r == 0, peep_tile, 0.0) + bias_tile

    small_step = [0] * 2
    small_moving = [None] * 2

    def small_next(i, tile=None):
        s = small_step[i]
        small_step[i] = s + 1
        while s < 4 and groups[s][0] == 1:
            s += 1
            small_step[i] = s + 1
        if tile is None:
            done = s - 1
            while groups[done][0] == 1:
                done -= 1
            for c in small_moving[i]:
                c.wait_recv()
            tile = small_bufs[done][i, 0]
            for k in range(1, groups[done][0]):
                tile = tile + small_bufs[done][i, k]
        if s < 4:
            size, peer, place = groups[s]
            ref = small_bufs[s].at[i, place]
            ref[...] = tile
            small_moving[i] = [remote(ref, ref, *peer(k)) for k in range(1, size)]
            return None
        return tile

    def small_finish(i):
        while True:
            tile = small_next(i)
            if tile is not None:
                return tile

    lanes = [(HALL, KALL), (0, WIDE), (WIDE, 2 * WIDE), (2 * WIDE, HALL)]
    steps = [0] * 4
    moving = [None] * 4

    def gather_low():
        if nlow > 1:
            low_send[...] = wt[far, mid, core]
            copies = [remote(low_send, low_recv.at[0, k - 1], *low_peer(k)) for k in range(1, nlow)]
            total = low_send[...]
            for k in range(1, nlow):
                copies[k - 1].wait_recv()
                total = total + low_recv[0, k - 1]
            wt[far, mid, core] = total

    def gather_step(i):
        lo, up = lanes[i]
        cols = pl.ds(lo, up - lo)
        s = steps[i]
        steps[i] = s + 1
        if 0 < s < 4:
            for c in moving[i]:
                c.wait_recv()
        if s < 3:
            g = (1, 0, 2)[s] if i == 1 else s
            size, peer, _ = groups[g]
            if s == 0:
                ref = wt.at[far, mid, core, :, cols]
            elif s == 1:
                ref = wt.at[far, :, core, :, cols] if i == 1 else wt.at[:, mid, core, :, cols]
            else:
                ref = wt.at[:, :, core, :, cols]
            moving[i] = [remote(ref, ref, *peer(k)) for k in range(1, size)]

    crop_h = crop_ref[0, 0]
    crop_w = crop_ref[0, 1]
    row0 = at_r * rows_n
    has_up = (at_r > 0).astype(F32)
    has_down = (at_r < nrow - 1).astype(F32)

    rr3 = lax.broadcasted_iota(jnp.int32, (CIN, rows_n, WID), 1) + row0
    cc3 = lax.broadcasted_iota(jnp.int32, (CIN, rows_n, WID), 2)
    live3 = (rr3 < crop_h) & (cc3 < crop_w)
    for t in range(frames_n):
        masked = jnp.where(live3, frames_ref[0, t].astype(F32), 0.0)
        fr[t, 1 : rows_n + 1] = jnp.swapaxes(masked, 0, 1)
        fhalo_s[0, t] = fr[t, 1].astype(BF16)
        fhalo_s[1, t] = fr[t, rows_n].astype(BF16)

    def lane_shift(v, by):
        at = lax.broadcasted_iota(jnp.int32, v.shape, 1)
        if by > 0:
            return jnp.where(at == WID - 1, 0.0, pltpu.roll(v, WID - 1, 1))
        return jnp.where(at == 0, 0.0, pltpu.roll(v, 1, 1))

    def row_shift(v, by):
        at = lax.broadcasted_iota(jnp.int32, v.shape, 0)
        if by > 0:
            return jnp.where(at == WID - 1, 0.0, pltpu.roll(v, WID - 1, 0))
        return jnp.where(at == 0, 0.0, pltpu.roll(v, 1, 0))

    def frame_part(t):
        return xt.at[t - 1, WIDE : WIDE + FEAT] if t > 0 else xt0

    def frame_cols(t, rr):
        v = fr[t, rr]
        three = jnp.concatenate([lane_shift(v, -1), v, lane_shift(v, 1)], axis=0)
        frame_part(t)[:, pl.ds(pl.multiple_of(rr * WID, WID), WID)] = three.astype(BF16)

    def frame_cols_all(rr, carry):
        for t in range(frames_n):
            frame_cols(t, rr)
        return carry

    def frame_pixels(t, lo, up):
        def one(rr, carry):
            parts = [
                frame_part(t)[:, pl.ds(pl.multiple_of((rr + a) * WID, WID), WID)].astype(F32)
                for a in range(3)
            ]
            parts.append(jnp.zeros((FPAD - 9 * CIN, WID), F32))
            gpre[t, pl.ds(pl.multiple_of(rr * WID, WID), WID), 0:FPAD] = (
                jnp.concatenate(parts, axis=0).T.astype(BF16)
            )
            return carry

        lax.fori_loop(lo, up, one, 0)

    lax.fori_loop(1, rows_n + 1, frame_cols_all, 0)
    frame_pixels(0, 1, rows_n - 1)

    pl.semaphore_wait(barrier, len(partners))
    gather_low()
    gather_step(0)
    gather_step(1)
    small_next(0, start_tile)
    f_up = remote(fhalo_s.at[0], fhalo_r.at[1], at_b, up_r)
    f_down = remote(fhalo_s.at[1], fhalo_r.at[0], at_b, down_r)
    gather_step(2)
    gather_step(3)
    if frames_n > 1:
        frame_pixels(1, 1, rows_n - 1)
    f_up.wait_recv()
    f_down.wait_recv()
    for t in range(frames_n):
        fr[t, 0] = fhalo_r[0, t].astype(F32) * has_up
        fr[t, rows_n + 1] = fhalo_r[1, t].astype(F32) * has_down
        frame_cols(t, 0)
        frame_cols(t, rows_n + 1)
    gather_step(1)
    gather_step(0)
    small_next(0)
    gather_step(2)
    for t in range(min(2, frames_n)):
        frame_pixels(t, 0, 1)
        frame_pixels(t, rows_n - 1, rows_n)
    gather_step(3)
    if frames_n > 2:
        frame_pixels(2, 0, rows_n)
    gather_step(0)
    small_next(0)
    for t in range(3, frames_n):
        frame_pixels(t, 0, rows_n)
    gather_step(0)

    consts[...] = small_finish(0)
    peep = [consts[i : i + 1, :] for i in range(3)]
    bias = [consts[4 + i : 5 + i, :] for i in range(4)]

    def cat_wt(lo, up):
        return wt[:, :, :, :, lo:up].reshape(GATES, up - lo)

    sub_iota = lax.broadcasted_iota(jnp.int32, (SUB, HID), 0)

    def live_cols(rr):
        return jnp.where(row0 + rr < crop_h, crop_w, 0)

    def place_state(t, v, at):
        three = [row_shift(v, -1), v, row_shift(v, 1)]
        for j in range(3):
            low_j = three[j].astype(BF16)
            sc[t, at, :, j * HID : (j + 1) * HID] = low_j
            xt[t, j * HID : (j + 1) * HID, at * WID : (at + 1) * WID] = low_j.T

    CH = 4
    nchunk = rows_n // CH

    def forward_dot(t, m):
        px = pl.ds(m * CH * WID, CH * WID)
        xf = gpre[t, px, 0:FPAD]
        if t > 0:
            parts = [sc[t - 1, m * CH + a : m * CH + a + CH].reshape(CH * WID, WIDE) for a in range(3)]
            x = jnp.concatenate(parts + [xf], axis=1)
            gates[t, px, :] = mm(x, cat_wt(0, KALL), NT)
        else:
            gates[t, px, :] = mm(xf, cat_wt(HALL, KALL), NT)

    def forward_rows(t, m):
        for rr in range(m * CH, (m + 1) * CH):
            limit = live_cols(rr)
            state = []
            for j in range(WID // SUB):
                sl = pl.ds(rr * WID + j * SUB, SUB)
                live = sub_iota + j * SUB < limit
                zi = gates[t, sl, 0:HID] + bias[0]
                zc = gates[t, sl, 2 * HID : 3 * HID] + bias[2]
                zo = gates[t, sl, 3 * HID :] + bias[3]
                if t > 0:
                    prev = cells[t - 1, sl, :]
                    zf = gates[t, sl, HID : 2 * HID] + bias[1] + peep[1] * prev
                    zi = zi + peep[0] * prev
                    gf = sigmoid(zf)
                    gates[t, sl, HID : 2 * HID] = gf
                gi = sigmoid(zi)
                gc = jnp.tanh(zc)
                c = gi * gc
                if t > 0:
                    c = c + gf * prev
                c = jnp.where(live, c, 0.0)
                go = sigmoid(zo + peep[2] * c)
                gates[t, sl, 0:HID] = gi
                gates[t, sl, 2 * HID : 3 * HID] = gc
                gates[t, sl, 3 * HID :] = go
                cells[t, sl, :] = c
                state.append(jnp.where(live, go * jnp.tanh(c), 0.0))
            state = jnp.concatenate(state, axis=0)
            if t < frames_n - 1:
                place_state(t, state, rr + 1)
            else:
                sc[0, rr + 1, :, 0:HID] = state.astype(BF16)

    hid_copies = []
    center = pl.ds(HID, HID)
    halos = [[None, None] for _ in range(frames_n)]

    def state_done(t, m):
        if t < frames_n - 1 and m == 0:
            halos[t][1] = remote(sc.at[t, 1, :, center], shalo_r.at[t, 1], at_b, up_r)
        if t < frames_n - 1 and m == nchunk - 1:
            halos[t][0] = remote(sc.at[t, rows_n, :, center], shalo_r.at[t, 0], at_b, down_r)
        if (t, m) == last_of[t]:
            lanes_of = center if t < frames_n - 1 else pl.ds(0, HID)
            src = sc.at[t if t < frames_n - 1 else 0, pl.ds(1, rows_n), :, lanes_of]
            c = pltpu.make_async_copy(src, hid_hbm.at[0, t], lsems.at[1 + t])
            c.start()
            hid_copies.append(c)

    inner = list(range(1, nchunk - 1))
    order = [inner + [nchunk - 1, 0], inner[::-1] + [0, nchunk - 1]]
    slots = [(0, m) for m in range(nchunk)] + [(t, m) for t in range(1, frames_n) for m in order[(t + 1) % 2]]
    last_of = {t: [s for s in slots if s[0] == t][-1] for t in range(frames_n)}
    for i, (t, m) in enumerate(slots + [(frames_n, 0)]):
        if t == 1 and m == order[0][0]:
            for k in range(1, 4):
                while steps[k] < 4:
                    gather_step(k)
        if 0 < t < frames_n and m == 0:
            halos[t - 1][0].wait_recv()
            place_state(t - 1, shalo_r[t - 1, 0].astype(F32) * has_up, 0)
        if 0 < t < frames_n and m == nchunk - 1:
            halos[t - 1][1].wait_recv()
            place_state(t - 1, shalo_r[t - 1, 1].astype(F32) * has_down, rows_n + 1)
        if t < frames_n:
            forward_dot(t, m)
        if i > 0:
            forward_rows(*slots[i - 1])
            state_done(*slots[i - 1])
        if t == 0 and 0 < m < 4:
            gather_step(m)

    cot_copy.wait()
    sums[...] = jnp.zeros_like(sums)

    def fold(v):
        return jnp.sum(v.reshape(SUB // 8, 8, HID), axis=0)

    def backward_rows(t, m):
        parts = [None] * 7
        for rr in range(m * CH, (m + 1) * CH):
            limit = live_cols(rr)
            for j in range(WID // SUB):
                cols = slice(j * SUB, (j + 1) * SUB)
                sl = pl.ds(rr * WID + j * SUB, SUB)
                live = sub_iota + j * SUB < limit
                gi = gates[t, sl, 0:HID]
                gc = gates[t, sl, 2 * HID : 3 * HID]
                go = gates[t, sl, 3 * HID :]
                c = cells[t, sl, :]
                sq = jnp.tanh(c)
                total = cot[t, rr, cols, :].astype(F32)
                if t < frames_n - 1:
                    total = total + gs[(t + 1) % 2, rr + 1, cols, :]
                    if rr == 0:
                        total = total + ghalo_r[t, 0, cols, :].astype(F32) * has_up
                    if rr == rows_n - 1:
                        total = total + ghalo_r[t, 1, cols, :].astype(F32) * has_down
                total = jnp.where(live, total, 0.0)
                tgo = total * go
                d_out = tgo * sq * (1.0 - go)
                nxt = tgo * (1.0 - sq * sq) + peep[2] * d_out
                if t < frames_n - 1:
                    nxt = nxt + cells[t + 1, sl, :]
                kept = jnp.where(live, nxt, 0.0)
                kgi = kept * gi
                d_in = kgi * gc * (1.0 - gi)
                d_cand = kgi * (1.0 - gc * gc)
                vals = [d_in, None, d_cand, d_out, None, None, d_out * c]
                if t > 0:
                    gf = gates[t, sl, HID : 2 * HID]
                    prev = cells[t - 1, sl, :]
                    kgf = kept * gf
                    d_for = kgf * prev * (1.0 - gf)
                    cells[t, sl, :] = kgf + peep[0] * d_in + peep[1] * d_for
                    vals[1] = d_for
                    vals[4] = d_in * prev
                    vals[5] = d_for * prev
                gpre[t, sl, 0:HID] = d_in.astype(BF16)
                gpre[t, sl, HID : 2 * HID] = (vals[1] if t > 0 else jnp.zeros_like(d_in)).astype(BF16)
                gpre[t, sl, 2 * HID : 3 * HID] = d_cand.astype(BF16)
                gpre[t, sl, 3 * HID :] = d_out.astype(BF16)
                for i in range(7):
                    if vals[i] is not None:
                        f = fold(vals[i])
                        parts[i] = f if parts[i] is None else parts[i] + f
        for i in range(7):
            if parts[i] is not None:
                sums[i] = sums[i] + parts[i]

    def state_chunk(t, m, done):
        y = mm(gpre[t, m * CH * WID : (m + 1) * CH * WID, :], cat_wt(0, HALL), NN)
        row = [None] * (CH + 2)
        for i in range(CH):
            for a in range(3):
                three = [y[i * WID : (i + 1) * WID, a * WIDE + j * HID : a * WIDE + (j + 1) * HID] for j in range(3)]
                z = three[1] + row_shift(three[0], 1) + row_shift(three[2], -1)
                row[i + a] = z if row[i + a] is None else row[i + a] + z
        for k in range(CH + 2):
            at = m * CH + k
            gs[t % 2, at] = gs[t % 2, at] + row[k] if at in done else row[k]
            done.add(at)

    work = [(t, m) for t in reversed(range(frames_n)) for m in order[(frames_n - 1 - t) % 2]]
    backward_rows(*work[0])
    ghalos = [[None, None] for _ in range(frames_n)]

    def rows_ready(t, m):
        if t < frames_n - 1 and m in (0, nchunk - 1):
            ghalos[t + 1][0 if m == 0 else 1].wait_recv()

    written = {t: set() for t in range(frames_n)}
    for i, (t, m) in enumerate(work):
        if t == 0:
            break
        rows_ready(*work[i + 1])
        state_chunk(t, m, written[t])
        backward_rows(*work[i + 1])
        if m == 0:
            ghalo_s[t - 1, 0] = gs[t % 2, 0].astype(BF16)
            ghalos[t][1] = remote(ghalo_s.at[t - 1, 0], ghalo_r.at[t - 1, 1], at_b, up_r)
        if m == nchunk - 1:
            ghalo_s[t - 1, 1] = gs[t % 2, rows_n + 1].astype(BF16)
            ghalos[t][0] = remote(ghalo_s.at[t - 1, 1], ghalo_r.at[t - 1, 0], at_b, down_r)
    left = work[-(nchunk - 1) :]

    stage = [0] * 4
    flight = [None] * 4
    last = len(PARTS) - 1
    def reduce_step(q):
        s = stage[q]
        stage[q] = s + 1
        first = acc[q][0]
        second = acc[q][1] if ncore > 1 else first.at[:, :, 0]
        if s == 0 and ncore > 1:
            core_send[q][...] = first[:, :, 1 - core].astype(BF16)
            flight[q] = [remote(core_send[q], core_recv[q], *core_peer(1))]
        elif s == 1:
            if ncore > 1:
                flight[q][0].wait_recv()
                second[...] = first[:, :, core] + core_recv[q][...].astype(F32)
            flight[q] = []
            if q >= DIRECT:
                tail_send[q - DIRECT][...] = second[...].astype(BF16)
                for k in range(1, nfar * nmid):
                    to = lax.rem(far * nmid + mid + k, nfar * nmid)
                    src = tail_send[q - DIRECT].at[to // nmid, to % nmid]
                    flight[q].append(remote(src, tail_recv[q - DIRECT].at[k - 1], *device(to // nmid, to % nmid, core, low)))
                return
            for k in range(1, nmid):
                to = lax.rem(mid + k, nmid)
                mid_send[q][k - 1] = second[:, to].astype(BF16)
                flight[q].append(remote(mid_send[q].at[k - 1], mid_recv[q].at[k - 1], *mid_peer(k)))
        elif s == 2 and q < DIRECT:
            total = second[:, mid]
            for k in range(1, nmid):
                flight[q][k - 1].wait_recv()
                total = total + mid_recv[q][k - 1].astype(F32)
            second[:, mid] = total
            far_send[q][...] = total.astype(BF16)
            flight[q] = []
            for k in range(1, nfar):
                to = lax.rem(far + k, nfar)
                flight[q].append(remote(far_send[q].at[to], far_recv[q].at[k - 1], *far_peer(k)))
        elif s == 3 or s == 2:
            stage[q] = 4
            total = second[far, mid]
            arrived = tail_recv[q - DIRECT] if q >= DIRECT else far_recv[q]
            for k in range(len(flight[q])):
                flight[q][k].wait_recv()
                total = total + arrived[k].astype(F32)
            a, lo, up, _ = PARTS[q]
            for j in range(3):
                at = (3 * a + j) * (CIN + HID)
                if up > WIDE:
                    nat[:, at : at + CIN] = total[:, WIDE - lo + j * CIN : WIDE - lo + (j + 1) * CIN]
                if lo <= j * HID < up:
                    nat[:, at + CIN : at + CIN + HID] = total[:, j * HID - lo : (j + 1) * HID - lo]

    def kernel_dot(q, t):
        a, lo, up, _ = PARTS[q]
        return mm(xt[t - 1, lo:up, a * WID : a * WID + pix], gpre[t], NN)

    def finish_rows(k):
        rows_ready(*left[k])
        backward_rows(*left[k])

    def place_part(q, total):
        a, lo, up, wide = PARTS[q]
        pieces = [total]
        if up > WIDE:
            pieces = [total[: WIDE - lo], total[WIDE - lo :] + fzero[a * FEAT : (a + 1) * FEAT, :]]
        if wide > up - lo:
            pieces.append(jnp.zeros((wide - up + lo, GATES), F32))
        acc[q][0][...] = jnp.concatenate(pieces, axis=0).T.reshape(acc[q][0].shape)

    after = {(1, 1): [0], (1, 2): [0], (2, 1): [1], (2, 2): [1], (3, 1): [2], (3, 2): [2]}
    totals = [None] * 4
    for q in range(4):
        for t in range(1, frames_n):
            part = kernel_dot(q, t)
            totals[q] = part if t == 1 else totals[q] + part
            if q == 0 and t - 1 < len(left):
                finish_rows(t - 1)
            if q > 0 and t == 1:
                place_part(q - 1, totals[q - 1])
            for k in after.get((q, t), []):
                reduce_step(k)
        if q == 0:
            for k in range(frames_n - 1, len(left)):
                finish_rows(k)
            g0 = [xt0[:, k * WID : k * WID + pix] for k in range(3)]
            fzero[...] = mm(jnp.concatenate(g0, axis=0), gpre[0], NN)
            rows = [jnp.sum(sums[i], axis=0, keepdims=True) for i in range(7)]
            small_next(1, jnp.concatenate(rows[4:] + [jnp.zeros((1, HID), F32)] + rows[:4], axis=0))
        elif q < 3:
            small_next(1)
    place_part(last, totals[last])
    reduce_step(last)
    reduce_step(0)

    fgb = fr

    def frame_back(t):
        y = mm(wft[0 : 9 * CIN, :], gpre[t], NT)
        row = [None] * (rows_n + 2)
        for i in range(rows_n):
            for a in range(3):
                part = y[a * FEAT : (a + 1) * FEAT, i * WID : (i + 1) * WID]
                z = part[CIN : 2 * CIN] + lane_shift(part[0:CIN], 1) + lane_shift(part[2 * CIN :], -1)
                row[i + a] = z if row[i + a] is None else row[i + a] + z
        for at in range(rows_n + 2):
            fgb[t, at] = row[at]
        bhalo_s[0, t] = row[0].astype(BF16)
        bhalo_s[1, t] = row[rows_n + 1].astype(BF16)

    wft[...] = cat_wt(HALL, KALL).astype(F32).T.astype(BF16)
    between = [[last], [], [1], [2]]
    for t in range(frames_n):
        frame_back(t)
        for q in between[t] if t < 4 else []:
            reduce_step(q)
    f_up = remote(bhalo_s.at[0], bhalo_r.at[1], at_b, up_r)
    f_down = remote(bhalo_s.at[1], bhalo_r.at[0], at_b, down_r)
    for q in (0, 3, 1, 2):
        while stage[q] < 4:
            reduce_step(q)
    if nlow > 1:
        low_send[...] = nat[...].astype(BF16)
        copies = [remote(low_send, low_recv.at[1, k - 1], *low_peer(k)) for k in range(1, nlow)]
        total = nat[...]
        for k in range(1, nlow):
            copies[k - 1].wait_recv()
            total = total + low_recv[1, k - 1].astype(F32)
        nat[...] = total

    g = nat[:, 0:KROWS]
    squares = g * g
    if nlow > 1:
        base = low * rows_own
        ri = lax.broadcasted_iota(jnp.int32, squares.shape, 0)
        squares = jnp.where((ri >= base) & (ri < base + rows_own), squares, 0.0)
    norm_tiles[me] = jnp.broadcast_to(jnp.sum(squares), (8, HID))

    def norm_copy(k):
        row = norm_tiles.at[me, 0:1]
        return pltpu.make_async_remote_copy(
            src_ref=row, dst_ref=row, send_sem=nsems.at[0, k], recv_sem=nsems.at[1, k],
            device_id=any_peer(k), device_id_type=MESH,
        )

    lax.fori_loop(1, ndev, lambda k, c: (norm_copy(k).start(), c)[1], 0)
    grad_ref[...] = g
    small = small_finish(1)
    small_out[...] = small
    f_up.wait_recv()
    f_down.wait_recv()
    for t in range(frames_n):
        fgb[t, 1] = fgb[t, 1] + bhalo_r[0, t].astype(F32) * has_up
        fgb[t, rows_n] = fgb[t, rows_n] + bhalo_r[1, t].astype(F32) * has_down
        fgo[t] = jnp.where(live3, jnp.swapaxes(fgb[t, 1 : rows_n + 1], 0, 1), 0.0)
    c = pltpu.make_async_copy(fgo, fg_hbm.at[0], lsems.at[1 + frames_n])
    c.start()
    hid_copies.append(c)
    for c in pending:
        c.wait_send()
    for c in hid_copies:
        c.wait()
    lax.fori_loop(1, ndev, lambda k, c: (norm_copy(k).wait_recv(), c)[1], 0)
    squares = jnp.sum(norm_tiles[:, 0:1, :], axis=0) + jnp.sum(small * small)
    norm_out[...] = jnp.broadcast_to(jnp.sqrt(squares), (8, HID))
    lax.fori_loop(1, ndev, lambda k, c: (norm_copy(k).wait_send(), c)[1], 0)


def adamw_update(weight, gradient, first, second, scale):
    clipped = gradient * scale
    first_new = BETA_ONE * first + (1.0 - BETA_ONE) * clipped
    second_new = BETA_TWO * second + (1.0 - BETA_TWO) * clipped * clipped
    first_hat = first_new / (1.0 - BETA_ONE**STEP)
    second_hat = second_new / (1.0 - BETA_TWO**STEP)
    weight_new = weight - LEARN_RATE * (
        first_hat / (jnp.sqrt(second_hat) + ADAM_EPS) + WEIGHT_DECAY * weight
    )
    return (weight_new, first_new, second_new)


def update_kernel(
    dims, hid_in, fg_in, norm_ref, sum_ref, small_ref,
    k_ref, b_ref, p_ref, k1_ref, k2_ref, b1_ref, b2_ref, p1_ref, p2_ref,
    hid_out, fg_out, norm_out, ko, k1o, k2o, bo, b1o, b2o, po, p1o, p2o, hid_buf, fg_buf, sems,
):
    nbat, nrow = dims
    frames_n = hid_buf.shape[0]
    fetch, put = [], []
    for t in range(frames_n):
        for i, (src, buf, dst) in enumerate(((hid_in, hid_buf, hid_out), (fg_in, fg_buf, fg_out))):
            fetch.append(pltpu.make_async_copy(src.at[0, t], buf.at[t], sems.at[i, t]))
            put.append(pltpu.make_async_copy(buf.at[t], dst.at[0, t], sems.at[2 + i, t]))
    for c in fetch:
        c.start()
    at_b = lax.axis_index("batch")
    at_r = lax.axis_index("rows")
    norm_out[0, 0] = norm_ref[0, 0]
    norm = jnp.full((1, HID), norm_ref[0, 0], F32)
    scale = jnp.minimum(1.0, CLIP_AT / (norm + 1e-06))
    small = small_ref[...]
    rows_own = b_ref.shape[1]
    peep_own = p_ref.shape[1]
    flat = (at_b * nrow + at_r) * rows_own
    lane_back = lax.rem(HID - flat % HID, HID)
    tile_row = lax.broadcasted_iota(jnp.int32, (8, HID), 0)
    picked = jnp.where(tile_row == 4 + flat // HID, small, 0.0)
    picked = jnp.sum(pltpu.roll(picked, lane_back, 1), axis=0, keepdims=True)
    new = adamw_update(b_ref[...], picked[:, 0:rows_own], b1_ref[...], b2_ref[...], scale[:, 0:rows_own])
    bo[...], b1o[...], b2o[...] = new
    shifted = pltpu.roll(small, lax.rem(HID - at_b * peep_own, HID), 1)
    new = adamw_update(p_ref[...], shifted[0:3, 0:peep_own], p1_ref[...], p2_ref[...], scale[:, 0:peep_own])
    po[...], p1o[...], p2o[...] = new
    new = adamw_update(k_ref[...], sum_ref[...], k1_ref[...], k2_ref[...], scale[:, 0:1])
    ko[...], k1o[...], k2o[...] = new
    for i in range(len(fetch)):
        fetch[i].wait()
        put[i].start()
    for c in put:
        c.wait()


def local(
    nbat,
    nrow,
    frames,
    crop_sizes,
    kernel,
    gate_bias,
    peepholes,
    cotangent,
    kernel_first,
    kernel_second,
    bias_first,
    bias_second,
    peep_first,
    peep_second,
):
    frames_n, rows_n = frames.shape[1], frames.shape[3]
    pix = rows_n * WID
    own = kernel.shape[1]
    nlow = max(1, UNIT // own)
    ncore = 2 if nrow > nlow else 1
    nmid = 2 * (nrow // (nlow * ncore))
    nfar = nbat // 2
    at_r = lax.axis_index("rows")

    kt = kernel.T
    if nlow > 1:
        kt = lax.dynamic_update_slice(
            jnp.zeros((UNIT, KROWS), F32), kt, (lax.rem(at_r, nlow) * own, 0)
        )
    bias_row = gate_bias.reshape(1, own)

    vm = pltpu.VMEM
    pair = (nfar, nmid) if ncore > 1 else (1, 1)
    wides = [(UNIT, part[3]) for part in PARTS]
    acc_shapes = [[vm((nfar, nmid, ncore) + wide, F32), vm(pair + wide, F32)] for wide in wides]
    ncopies = (
        2 * (nfar + nmid + ncore + nlow - 4)
        + 4 * (nfar + nmid + ncore - 3)
        + DIRECT * (nfar + nmid - 2)
        + len(PARTS) * (ncore - 1)
        + (len(PARTS) - DIRECT) * (nfar * nmid - 1)
        + 4
        + 4 * (frames_n - 1)
        + 2 * (nlow - 1)
    )
    scratch = [
        vm((nfar, nmid, ncore, UNIT, KALL), BF16),
        vm((FPAD, GATES), BF16),
        vm((frames_n, rows_n + 2, CIN, WID), F32),
        vm((frames_n - 1, WIDE + FEAT, (rows_n + 2) * WID), BF16),
        vm((FEAT, (rows_n + 2) * WID), BF16),
        vm((frames_n - 1, rows_n + 2, WID, WIDE), BF16),
        vm((frames_n, pix, GATES), F32),
        vm((frames_n, pix, HID), F32),
        vm((frames_n, pix, GATES), BF16),
        vm((2, rows_n + 2, WID, HID), F32),
        vm((frames_n, rows_n, WID, HID), BF16),
        vm((8, HID), F32),
        vm((7, 8, HID), F32),
        acc_shapes,
        vm((9 * CIN, GATES), F32),
        vm((frames_n, CIN, rows_n, WID), F32),
        vm((2, frames_n, CIN, WID), BF16),
        vm((2, frames_n, CIN, WID), BF16),
        vm((frames_n - 1, 2, WID, HID), BF16),
        vm((frames_n - 1, 2, WID, HID), BF16),
        vm((frames_n - 1, 2, WID, HID), BF16),
        vm((2, frames_n, CIN, WID), BF16),
        vm((2, frames_n, CIN, WID), BF16),
        vm((UNIT, KALL), F32),
    ]
    scratch += [vm(pair + wide, BF16) for wide in wides + wides]
    two = [wide if q < DIRECT else (8, HID) for q, wide in enumerate(wides)]
    mids = [(nmid - 1, nfar) if q < DIRECT else (1, 1) for q in range(len(two))]
    fars = [(nfar,) if q < DIRECT else (1,) for q in range(len(two))]
    scratch += [vm(mids[q] + two[q], BF16) for q in range(len(two))] * 2
    scratch += [vm(fars[q] + two[q], BF16) for q in range(len(two))] * 2
    scratch += [vm((2, size, 8, HID), F32) for size in (nfar, nmid, ncore, nlow)]
    scratch += [vm((nfar, nmid) + wide, BF16) for wide in wides[DIRECT:]]
    scratch += [vm((nfar * nmid - 1,) + wide, BF16) for wide in wides[DIRECT:]]
    scratch += [vm((UNIT, KALL), BF16), vm((2, max(1, nlow - 1), UNIT, KALL), BF16)]
    scratch += [vm((nbat * nrow, 8, HID), F32), pltpu.SemaphoreType.DMA((2, nbat * nrow))]
    scratch += [
        pltpu.SemaphoreType.DMA((ncopies,)),
        pltpu.SemaphoreType.DMA((ncopies,)),
        pltpu.SemaphoreType.DMA((2 + frames_n,)),
    ]
    smem = pl.BlockSpec(memory_space=pltpu.SMEM)
    vmem = pl.BlockSpec(memory_space=pltpu.VMEM)
    hbm = pl.BlockSpec(memory_space=pl.ANY)
    dims = (nbat, nrow, frames_n, rows_n, nfar, nmid, ncore, nlow)
    hidden, frames_back, kernel_sum, small_sum, norm = pl.pallas_call(
        functools.partial(layer_kernel, dims),
        out_shape=(
            jax.ShapeDtypeStruct(cotangent.shape, BF16),
            jax.ShapeDtypeStruct(frames.shape, F32),
            jax.ShapeDtypeStruct((UNIT, KROWS), F32),
            jax.ShapeDtypeStruct((8, HID), F32),
            jax.ShapeDtypeStruct((8, HID), F32),
        ),
        in_specs=[smem, vmem, vmem, vmem, vmem, hbm],
        out_specs=(hbm, hbm, vmem, vmem, vmem),
        scratch_shapes=scratch,
        compiler_params=pltpu.CompilerParams(
            collective_id=0, has_side_effects=True, vmem_limit_bytes=63 << 20
        ),
        name="layer",
    )(crop_sizes, frames, kt, bias_row, peepholes, cotangent)

    if nlow > 1:
        kernel_sum = lax.dynamic_slice_in_dim(kernel_sum, lax.rem(at_r, nlow) * own, own, 0)
    kshape = jax.ShapeDtypeStruct((own, KROWS), F32)
    bshape = jax.ShapeDtypeStruct((1, own), F32)
    pshape = jax.ShapeDtypeStruct(peepholes.shape, F32)
    outs = pl.pallas_call(
        functools.partial(update_kernel, (nbat, nrow)),
        out_shape=(
            jax.ShapeDtypeStruct(cotangent.shape, BF16),
            jax.ShapeDtypeStruct(frames.shape, F32),
            jax.ShapeDtypeStruct((1, 1), F32),
        )
        + (kshape,) * 3 + (bshape,) * 3 + (pshape,) * 3,
        in_specs=[hbm, hbm, smem] + [vmem] * 11,
        out_specs=(hbm, hbm, smem) + (vmem,) * 9,
        scratch_shapes=[
            pltpu.VMEM(cotangent.shape[1:], BF16),
            pltpu.VMEM(frames.shape[1:], F32),
            pltpu.SemaphoreType.DMA((4, frames_n)),
        ],
        compiler_params=pltpu.CompilerParams(vmem_limit_bytes=63 << 20),
        name="update",
    )(
        hidden, frames_back, norm, kernel_sum, small_sum,
        kernel.T, bias_row, peepholes, kernel_first.T, kernel_second.T,
        bias_first.reshape(1, own), bias_second.reshape(1, own), peep_first, peep_second,
    )
    hidden_seq, frames_grad, norm = outs[:3]
    kernels, biases, peeps = outs[3:6], outs[6:9], outs[9:]
    return (
        hidden_seq,
        frames_grad,
        norm[0, 0],
        *(k.T for k in kernels),
        *(v.reshape(own) for v in biases),
        *peeps,
    )


def solution(mesh):
    return jax.shard_map(
        functools.partial(local, mesh.shape["batch"], mesh.shape["rows"]),
        mesh=mesh,
        in_specs=(
            P("batch", None, None, "rows", None),
            P("batch", None),
            P(None, ("batch", "rows")),
            P(("batch", "rows")),
            P(None, "batch"),
            P("batch", None, "rows", None, None),
            P(None, ("batch", "rows")),
            P(None, ("batch", "rows")),
            P(("batch", "rows")),
            P(("batch", "rows")),
            P(None, "batch"),
            P(None, "batch"),
        ),
        out_specs=(
            P("batch", None, "rows", None, None),
            P("batch", None, None, "rows", None),
            P(),
            P(None, ("batch", "rows")),
            P(None, ("batch", "rows")),
            P(None, ("batch", "rows")),
            P(("batch", "rows")),
            P(("batch", "rows")),
            P(("batch", "rows")),
            P(None, "batch"),
            P(None, "batch"),
            P(None, "batch"),
        ),
        check_vma=False,
    )
```
